512 devices in a mesh: node: 32 (over z, x), ens: 4 (over y_lo), dp: 4 (over y_hi, core).
Axes of the slice: x: 4, y: 8 (y_hi: 2, y_lo: 4; y = y_hi * 4 + y_lo), z: 8, core: 2. Of those that a mesh axis runs over, the one named last changes fastest.
Arguments:
- nodes: bfloat16 [4, 4, 4096, 1024], P('dp', 'ens', 'node'), may hold values from -6 to 6
- w_query: bfloat16 [1024, 1024], P('node'), may hold values from -0.1875 to 0.1875
- w_key: bfloat16 [1024, 1024], P('node'), may hold values from -0.1875 to 0.1875
- w_value: bfloat16 [1024, 1024], P('node'), may hold values from -0.1875 to 0.1875
- w_output: bfloat16 [1024, 1024], P('node'), may hold values from -0.1875 to 0.1875
- w_head: bfloat16 [1024, 128], P('node'), may hold values from -0.25 to 0.25
- neighbours: int32 [4096, 16], P('node'), may hold values from 0 to 4095, as said below
- edge_counts: int32 [4096], P('node'), may hold values from 1 to 16
- target: float32 [4, 4096, 128], P('dp', 'node'), may hold values from -6 to 6
- node_area: float32 [4096], P('node'), may hold values from 1 to 10
Outputs:
- grad_nodes: bfloat16 [4, 4, 4096, 1024], P('dp', 'ens', 'node')
- grad_out_proj: float32 [1048576], P(('node', 'ens', 'dp'))
The draws below stay inside these ranges and needn't reach their ends.
Inputs may be any that keep to these rules, and one draw needn't show every extreme that they name: `neighbours`: row i lists 16 different nodes: slot 0 is i itself and every other slot is (i + o) mod 4096 with 1 <= |o| <= 32. Slot s of node i's list is an edge where s < edge_counts[i].
All inputs are finite; a program needn't handle non-finite values.
Results may differ from the reference program's by a relative error of at most 0.015.
Values may be sent and summed in bfloat16 or wider, within the bound.
A program may use at most 64 MiB of HBM per device.

```python
import math
import jax
import jax.numpy as jnp
from jax import lax

D = 1024
HEADS = 16
NV = 128
K = 16
NB = 128
NODES = 4096
MEMBERS = 4
DATES = 4
N_NODE = 32


def draw_neighbours(key, part):
    key = jax.random.fold_in(key, 11)
    reach_rows = NB // 4
    offsets = jnp.concatenate([jnp.arange(-reach_rows, 0, dtype=jnp.int32), jnp.arange(1, reach_rows + 1, dtype=jnp.int32)])
    row_keys = jax.random.split(key, NODES)

    def pick_offsets(row_key):
        return jax.random.permutation(row_key, offsets)[:K - 1]
    chosen = jax.vmap(pick_offsets)(row_keys)
    picked = jnp.concatenate([jnp.zeros((NODES, 1), jnp.int32), chosen], axis=1)
    node_index = jnp.arange(NODES, dtype=jnp.int32)[:, None]
    return ((node_index + picked) % NODES).astype(jnp.int32)


def touch_ends(drawn, rng, smallest, largest):
    index_at = [jax.random.randint(jax.random.fold_in(rng, axis), (), 0, length) for axis, length in enumerate(drawn.shape)]
    main_axis = drawn.shape.index(max(drawn.shape))
    neighbour = index_at[:main_axis] + [(index_at[main_axis] + 1) % drawn.shape[main_axis]] + index_at[main_axis + 1:]
    return drawn.at[tuple(index_at)].set(smallest).at[tuple(neighbour)].set(largest)


def levels(rng, dims, cuts, smallest, top_value):
    factor_of, own = 1.0, jax.random.fold_in(rng, 6)
    for dim, parts in cuts:
        draws = jnp.exp(jax.random.uniform(jax.random.fold_in(own, dim), (parts,), jnp.float32, smallest / len(cuts), top_value / len(cuts)))
        factor_of = factor_of * jnp.repeat(draws, dims[dim] // parts).reshape([-1 if axis == dim else 1 for axis in range(len(dims))])
    return factor_of


def noise(key, extent, scale, most, cuts=(), kind=jnp.bfloat16):
    entries = jax.random.normal(key, extent, jnp.float32) * scale
    if len(cuts) > 0:
        entries = levels(key, extent, cuts, -0.22, 0.18) * entries
    return jnp.clip(entries, min=-most, max=most).astype(kind)


def setup_inputs(seed: int = 0) -> dict:
    streams_of = jax.random.split(jax.random.key(seed), 11)
    nodes = noise(streams_of[0], (DATES, MEMBERS, NODES, D), 1.0, 6.0, ((0, 4), (1, 4), (2, 32)))
    w_query = noise(streams_of[1], (D, D), D ** -0.5, 0.1875, ((0, 32),))
    w_key = noise(streams_of[2], (D, D), D ** -0.5, 0.1875, ((0, 32),))
    w_value = noise(streams_of[3], (D, D), D ** -0.5, 0.1875, ((0, 32),))
    w_output = noise(streams_of[4], (D, D), D ** -0.5, 0.1875, ((0, 32),))
    w_head = noise(streams_of[5], (D, NV), (4 * NV) ** -0.5, 0.25, ((0, 32),))
    neighbours = draw_neighbours(jax.random.fold_in(streams_of[10], 71), 0)
    edge_counts = touch_ends(jax.random.randint(streams_of[7], (NODES,), 1, K + 1), jax.random.fold_in(streams_of[7], 1), 1, K).astype(jnp.int32)
    target = noise(streams_of[8], (DATES, NODES, NV), 1.0, 6.0, ((0, 4), (1, 32)), jnp.float32)
    node_area = jnp.clip(jnp.exp(math.log(10.0) - 2.3025851 * jax.random.uniform(streams_of[9], (NODES,), jnp.float32) ** levels(streams_of[9], (NODES,), ((0, 32),), -0.2, 0.2)), 1.0, 10.0)
    return {"nodes": nodes, "w_query": w_query, "w_key": w_key, "w_value": w_value, "w_output": w_output, "w_head": w_head, "neighbours": neighbours, "edge_counts": edge_counts, "target": target, "node_area": node_area}


fair_weight = 0.95
soft_square = 0.25

def to_half(values):
    return lax.optimization_barrier(values.astype(jnp.bfloat16))

def widen(values):
    return values.astype(jnp.float32)

def layer_norm(inputs):
    values = inputs.astype(jnp.float32)
    centre = lax.optimization_barrier(jnp.mean(values, axis=-1, keepdims=True))
    shifted = values - centre
    factor = lax.rsqrt(lax.optimization_barrier(jnp.mean(shifted * shifted, axis=-1, keepdims=True)) + 1e-05)
    return (shifted * factor, factor)

def layer_norm_back(grad_in, normal, factor):
    centre = lax.optimization_barrier(jnp.mean(grad_in, axis=-1, keepdims=True))
    along = lax.optimization_barrier(jnp.mean(grad_in * normal, axis=-1, keepdims=True))
    return factor * (grad_in - centre - normal * along)

def head_norm(values, head_count):
    grouped = values.reshape(values.shape[0], head_count, values.shape[1] // head_count)
    factor = lax.rsqrt(lax.optimization_barrier(jnp.mean(grouped * grouped, axis=-1, keepdims=True)) + 1e-06)
    return (grouped * factor, factor)

def head_norm_back(grad_in, normal, factor):
    along = lax.optimization_barrier(jnp.mean(grad_in * normal, axis=-1, keepdims=True))
    return factor * (grad_in - normal * along)

def soft_sign(values):
    return values * lax.rsqrt(values * values + soft_square)

def matmul(left, right):
    return jnp.dot(left, right, preferred_element_type=jnp.float32)

def matmul_back(left, right):
    return lax.dot_general(left, right, (((1,), (1,)), ((), ())), preferred_element_type=jnp.float32)

def edge_attention(query_block, key_half, neigh_block, count_block):
    near_keys = widen(key_half[neigh_block])
    scores = jnp.einsum('rhd,rkhd->rhk', widen(query_block), near_keys, precision=lax.Precision.HIGHEST) / math.sqrt(D // HEADS)
    valid = (jnp.arange(K, dtype=jnp.int32)[None, :] < count_block[:, None]).astype(jnp.float32)
    raised = jnp.exp(scores) * valid[:, None, :]
    return (raised / lax.optimization_barrier(jnp.sum(raised, axis=-1, keepdims=True)), near_keys)

def forward_pieces(graph_nodes, weights, neighbours, edge_counts):
    w_query, w_key, w_value, w_output, w_head = weights
    head_size = D // HEADS
    normal, factor = layer_norm(graph_nodes)
    normed = to_half(normal)
    query_unit, query_factor = head_norm(matmul(normed, w_query), HEADS)
    key_unit, key_factor = head_norm(matmul(normed, w_key), HEADS)
    query_half = to_half(query_unit)
    key_half = to_half(key_unit)
    value_half = to_half(matmul(normed, w_value)).reshape(NODES, HEADS, head_size)

    def block_mix(block):
        first = (block * NB).astype(jnp.int32)
        query_block = lax.dynamic_slice_in_dim(query_half, first, NB, 0)
        neigh_block = lax.dynamic_slice_in_dim(neighbours, first, NB, 0)
        count_block = lax.dynamic_slice_in_dim(edge_counts, first, NB, 0)
        attention, near_keys = edge_attention(query_block, key_half, neigh_block, count_block)
        near_values = widen(value_half[neigh_block])
        mixed = jnp.einsum('rhk,rkhd->rhd', widen(to_half(attention)), near_values, precision=lax.Precision.HIGHEST)
        return to_half(mixed)
    mixed = lax.map(block_mix, jnp.arange(N_NODE, dtype=jnp.int32)).reshape(NODES, D)
    settled = to_half(widen(graph_nodes) + matmul(mixed, w_output))
    return (normal, factor, query_unit, query_factor, key_unit, key_factor, query_half, key_half, value_half, mixed, settled)

def graph_backward(graph_nodes, weights, neighbours, edge_counts, grad_pred):
    w_query, w_key, w_value, w_output, w_head = weights
    head_size = D // HEADS
    normal, factor, query_unit, query_factor, key_unit, key_factor, query_half, key_half, value_half, mixed, settled = forward_pieces(graph_nodes, weights, neighbours, edge_counts)
    grad_settled = to_half(matmul_back(grad_pred, w_head))
    out_grad = lax.dot_general(mixed, grad_settled, (((0,), (0,)), ((), ())), preferred_element_type=jnp.float32)
    grad_mixed = to_half(matmul_back(grad_settled, w_output)).reshape(NODES, HEADS, head_size)

    def block_back(carry, block):
        key_sum, value_sum = carry
        first = (block * NB).astype(jnp.int32)
        query_block = lax.dynamic_slice_in_dim(query_half, first, NB, 0)
        neigh_block = lax.dynamic_slice_in_dim(neighbours, first, NB, 0)
        count_block = lax.dynamic_slice_in_dim(edge_counts, first, NB, 0)
        grad_block = widen(lax.dynamic_slice_in_dim(grad_mixed, first, NB, 0))
        attention, near_keys = edge_attention(query_block, key_half, neigh_block, count_block)
        near_values = widen(value_half[neigh_block])
        grad_scores = jnp.einsum('rhd,rkhd->rhk', grad_block, near_values, precision=lax.Precision.HIGHEST)
        grad_logits = widen(to_half(attention * (grad_scores - lax.optimization_barrier(jnp.sum(attention * grad_scores, axis=-1, keepdims=True)))))
        query_grad = jnp.einsum('rhk,rkhd->rhd', grad_logits, near_keys, precision=lax.Precision.HIGHEST) / math.sqrt(head_size)
        key_terms = jnp.einsum('rhk,rhd->rkhd', grad_logits, widen(query_block), precision=lax.Precision.HIGHEST) / math.sqrt(head_size)
        value_terms = jnp.einsum('rhk,rhd->rkhd', widen(to_half(attention)), grad_block, precision=lax.Precision.HIGHEST)
        return ((key_sum.at[neigh_block].add(key_terms), value_sum.at[neigh_block].add(value_terms)), query_grad)
    empty = jnp.zeros((NODES, HEADS, head_size), jnp.float32)
    (key_grad, value_grad), query_grad = lax.scan(block_back, (empty, empty), jnp.arange(N_NODE, dtype=jnp.int32))
    query_grad = query_grad.reshape(NODES, HEADS, head_size)
    grad_query = to_half(head_norm_back(query_grad, query_unit, query_factor)).reshape(NODES, D)
    grad_key = to_half(head_norm_back(key_grad, key_unit, key_factor)).reshape(NODES, D)
    grad_value = to_half(value_grad).reshape(NODES, D)
    grad_normed = matmul_back(grad_query, w_query) + matmul_back(grad_key, w_key) + matmul_back(grad_value, w_value)
    grad_nodes = widen(grad_settled) + layer_norm_back(grad_normed, normal, factor)
    return (grad_nodes.astype(jnp.bfloat16), out_grad)

def prediction_grad(predicted, target, node_area):
    members = predicted.shape[1]
    coefficient = fair_weight / (2 * members * (members - 1)) + (1 - fair_weight) / (2 * members * members)
    differ = predicted - target[:, None]
    paired = jnp.zeros_like(differ)
    for other in range(members):
        paired = paired + soft_sign(differ - differ[:, other:other + 1])
    core = soft_sign(differ) / members - 2 * coefficient * paired
    return (node_area[None, None, :, None] * core).astype(jnp.bfloat16)

def reference(nodes, w_query, w_key, w_value, w_output, w_head, neighbours, edge_counts, target, node_area):
    weights = (w_query, w_key, w_value, w_output, w_head)
    graphs = nodes.reshape(DATES * MEMBERS, NODES, D)

    def predict_graph(graph_nodes):
        pieces = forward_pieces(graph_nodes, weights, neighbours, edge_counts)
        return matmul(pieces[-1], w_head)
    predicted = lax.map(predict_graph, graphs).reshape(DATES, MEMBERS, NODES, NV)
    grad_pred = prediction_grad(predicted, target, node_area).reshape(DATES * MEMBERS, NODES, NV)

    def backward_graph(summed, inputs_pair):
        grad_graph, out_grad = graph_backward(inputs_pair[0], weights, neighbours, edge_counts, inputs_pair[1])
        return (summed + out_grad, grad_graph)
    summed, grad_nodes = lax.scan(backward_graph, jnp.zeros((D, D), jnp.float32), (graphs, grad_pred))
    return (grad_nodes.reshape(DATES, MEMBERS, NODES, D), summed.reshape(D * D))
```

```python
import jax
import jax.numpy as jnp
from jax import lax
from jax.experimental import pallas as pl
from jax.experimental.pallas import tpu as pltpu
from jax.sharding import PartitionSpec as P

HEADS = 16


fair_weight = 0.95
soft_square = 0.25

NZ, NX, NY = 8, 4, 8
MESH = pl.DeviceIdType.MESH


def place():
    node = lax.axis_index("node")
    ens = lax.axis_index("ens")
    dp = lax.axis_index("dp")
    return node // NX, node % NX, (dp // 2) * 4 + ens, dp % 2


def at(z, x, y, core):
    return {"node": z * NX + x, "ens": y % 4, "dp": (y // 4) * 2 + core}


class Sender:
    def __init__(self, sems):
        self.sems, self.count, self.sent = sems, 0, []

    def start(self, src, dst, recv_sem, device):
        copy = pltpu.make_async_remote_copy(
            src_ref=src,
            dst_ref=dst,
            send_sem=self.sems.at[self.count],
            recv_sem=recv_sem,
            device_id=device,
            device_id_type=MESH,
        )
        self.count += 1
        copy.start()
        self.sent.append(copy)

    def finish(self):
        for copy in self.sent:
            copy.wait_send()
        self.sent = []


def landed(region, sem):
    pltpu.make_async_copy(region, region, sem).wait()


def greet(peers):
    barrier = pltpu.get_barrier_semaphore()
    for peer in peers:
        pl.semaphore_signal(barrier, inc=1, device_id=peer, device_id_type=MESH)
    pl.semaphore_wait(barrier, len(peers))


TILE = 256
HALO = 32
EXT = 256
FIRST = 1024


def spread(z):
    return (z + 2 * NZ) % NZ


class Gather:
    def __init__(self, whole, sender, recv, pair):
        self.whole, self.sender, self.recv, self.pair = whole, sender, recv, pair
        self.z, self.x, self.y, self.core = place()
        z, x, y, core = self.z, self.x, self.y, self.core
        self.half = pl.ds(pl.multiple_of(core * 16, 16), 16)
        self.near = [at(z, (x + d) % NX, y, core) for d in (1, 2, 3)]
        self.up = at((z + 1) % NZ, x, y, core)
        self.down = at((z + NZ - 1) % NZ, x, y, core)
        self.twin = at(z, x, y, 1 - core)

    def send(self, region, sem, peer):
        self.sender.start(region, region, self.recv.at[sem], peer)

    def share(self, region):
        self.sender.start(region, region, self.pair, self.twin)

    def paired(self):
        landed(self.whole.at[:, :, pl.ds(0, 16)], self.pair)

    def own(self, columns):
        return self.whole.at[self.z, self.x, self.half, columns]

    def line(self, dz, columns):
        return self.whole.at[spread(self.z + dz), :, self.half, columns]

    def one(self, dz, columns):
        return self.whole.at[spread(self.z + dz), self.x, self.half, columns]

    def across(self, columns, base):
        for d in range(3):
            self.send(self.own(columns), base + d, self.near[d])

    def crossed(self, columns, base):
        for d in (1, 2, 3):
            region = self.whole.at[
                self.z, (self.x - d + NX) % NX, self.half, columns
            ]
            landed(region, self.recv.at[base + d - 1])

    def pass_crossed(self, columns):
        for d in (1, 2, 3):
            self.share(
                self.whole.at[self.z, (self.x - d + NX) % NX, self.half, columns]
            )

    def ring_begin(self, block, columns, base):
        self.send(block(0, columns), base, self.up)
        self.send(block(0, columns), base + 4, self.down)

    def ring_step(self, block, columns, base, s, shared=True):
        low, high = block(-s, columns), block(s, columns)
        landed(low, self.recv.at[base + s - 1])
        if s < 4:
            self.send(low, base + s, self.up)
            landed(high, self.recv.at[base + s + 3])
            if s < 3:
                self.send(high, base + s + 4, self.down)
        if shared:
            self.share(low)
            if s < 4:
                self.share(high)

    def column(self, dx, z0, count, columns):
        x = (self.x + dx + NX) % NX
        return self.whole.at[pl.ds(z0, count), x, self.half, columns]

    def column_begin(self, columns, base):
        region = self.column(0, 0, NZ, columns)
        self.send(region, base, self.near[0])
        self.send(region, base + 1, self.near[2])

    def column_step(self, columns, base):
        for sem, dx, z0, peer in (
            (base, -1, 0, self.near[0]),
            (base + 1, 1, 4, self.near[2]),
        ):
            region = self.column(dx, 0, NZ, columns)
            landed(region, self.recv.at[sem])
            self.send(self.column(dx, z0, 4, columns), sem + 2, peer)
            self.share(region)

    def column_end(self, columns, base):
        for sem, z0 in ((base + 2, 0), (base + 3, 4)):
            region = self.column(2, z0, 4, columns)
            landed(region, self.recv.at[sem])
            self.share(region)

    def slab(self, dy):
        width = self.whole.shape[3] // NY
        first = pl.multiple_of(((self.y + dy + NY) % NY) * width, width)
        return self.whole.at[:, :, self.half, pl.ds(first, width)]

    def y_begin(self, base):
        self.share(self.slab(0))
        y, core = self.y, self.core
        self.send(self.slab(0), base, at(self.z, self.x, (y + 1) % NY, core))
        self.send(self.slab(0), base + 4, at(self.z, self.x, (y + NY - 1) % NY, core))

    def y_step(self, base, s):
        y, core = self.y, self.core
        low, high = self.slab(-s), self.slab(s)
        landed(low, self.recv.at[base + s - 1])
        if s < 4:
            self.send(low, base + s, at(self.z, self.x, (y + 1) % NY, core))
            landed(high, self.recv.at[base + s + 3])
            if s < 3:
                self.send(
                    high, base + s + 4, at(self.z, self.x, (y + NY - 1) % NY, core)
                )
        self.share(low)
        if s < 4:
            self.share(high)


def all_peers():
    z, x, y, core = place()
    node = z * NX + x
    peers = [at(z, (x + d) % NX, y, core) for d in range(1, NX)]
    peers += [at((z + d) % NZ, x, y, core) for d in range(1, NZ)]
    for dy in range(NY):
        for dc in range(2):
            if dy or dc:
                peers.append(at(z, x, (y + dy) % NY, (core + dc) % 2))
    peers.append({"node": (node + 1) % (NZ * NX)})
    peers.append({"node": (node + NZ * NX - 1) % (NZ * NX)})
    return peers


def mat(left, right):
    return jnp.dot(left, right, preferred_element_type=jnp.float32)


def mat_back(left, right):
    return lax.dot_general(
        left, right, (((1,), (1,)), ((), ())), preferred_element_type=jnp.float32
    )


def mat_across(left, right):
    return lax.dot_general(
        left, right, (((0,), (0,)), ((), ())), preferred_element_type=jnp.float32
    )


def soft_sign(values):
    return values * lax.rsqrt(values * values + soft_square)


def lane(start, size):
    return pl.ds(pl.multiple_of(start, size), size)


def head_side():
    return lax.broadcasted_iota(jnp.int32, (1, 128), 1) < 64


def head_mean(values):
    side = head_side()
    low = jnp.sum(jnp.where(side, values, 0.0), axis=1, keepdims=True)
    high = jnp.sum(jnp.where(side, 0.0, values), axis=1, keepdims=True)
    return jnp.where(side, low, high) * (1.0 / 64)


def two_heads(values):
    side = head_side()
    empty = jnp.zeros_like(values)
    return jnp.where(side, values, empty), jnp.where(side, empty, values)


def layer_kernel(
    nodes, wq_shard, wk_shard, wv_shard, wo_shard, wh_shard, neighbours, counts,
    target, area, out, out_sum,
    wqkv, wo, wh, normal, normed, factor, q_unit, k_unit, q_factor, k_factor, q_half,
    kv, near, attention, left, right, settled, differ, differs, gs, gm, gq, dk, dv,
    gk, gv, gn, halo_out, halo_in, parts, from_x, halves, from_z, pieces, from_y,
    local, send, recv_a, recv_o, recv_h, pair, halo_send, halo_recv, back_recv,
    ens_recv, recv_core, recv_x, recv_z, recv_y,
):
    f32, half = jnp.float32, jnp.bfloat16
    z, x, y, core = place()
    node = z * NX + x
    rows, width = nodes.shape
    sender = Sender(send)
    own_half = pl.ds(pl.multiple_of(core * 16, 16), 16)
    loads = []
    slab = pl.ds(pl.multiple_of(y * 128, 128), 128)
    all_columns = pl.ds(0, width)
    every_h = pl.ds(0, wh_shard.shape[1])
    for k, (shard, whole, taken, kept) in enumerate(
        (
            (wq_shard, wqkv, all_columns, pl.ds(0, width)),
            (wk_shard, wqkv, all_columns, pl.ds(width, width)),
            (wv_shard, wqkv, all_columns, pl.ds(2 * width, width)),
            (wo_shard, wo, slab, slab),
            (wh_shard, wh, every_h, every_h),
        )
    ):
        load = pltpu.make_async_copy(
            shard.at[own_half, taken],
            whole.at[z, x, own_half, kept],
            local.at[k],
        )
        load.start()
        loads.append(load)
    greet(all_peers())
    for load in loads:
        load.wait()

    ga = Gather(wqkv, sender, recv_a, pair.at[0])
    go = Gather(wo, sender, recv_o, pair.at[1])
    gh = Gather(wh, sender, recv_h, pair.at[2])
    first, last = pl.ds(0, FIRST), pl.ds(FIRST, 3 * width - FIRST)
    ga.across(last, 0)
    ga.ring_begin(ga.one, first, 3)
    go.across(slab, 0)
    gh.across(every_h, 0)
    ga.share(ga.own(pl.ds(0, 3 * width)))
    gh.share(gh.own(every_h))

    values = nodes[...].astype(f32)
    shifted = values - jnp.mean(values, axis=1, keepdims=True)
    scale = lax.rsqrt(jnp.mean(shifted * shifted, axis=1, keepdims=True) + 1e-05)
    factor[...] = jnp.broadcast_to(scale, factor.shape)
    normal[...] = shifted * scale
    normed[...] = normal[...].astype(half)

    ga.crossed(last, 0)
    ga.ring_begin(ga.line, last, 10)
    ga.ring_step(ga.one, first, 3, 1)
    go.crossed(slab, 0)
    go.ring_begin(go.line, slab, 3)
    gh.crossed(every_h, 0)
    gh.ring_begin(gh.line, every_h, 3)
    ga.pass_crossed(last)
    gh.pass_crossed(every_h)

    column = (
        neighbours[...] - node * rows + HALO + NZ * NX * rows
    ) & (NZ * NX * rows - 1)
    at_column = lax.broadcasted_iota(jnp.int32, (rows, EXT), 1)
    hits = jnp.zeros((rows, EXT), f32)
    for s in range(neighbours.shape[1]):
        hit = (column[:, s : s + 1] == at_column) & (counts[...] > s)
        hits = hits + jnp.where(hit, 1.0, 0.0)
    near[...] = hits
    kv[:, pl.ds(rows + 2 * HALO, EXT - rows - 2 * HALO)] = jnp.zeros(
        (2, EXT - rows - 2 * HALO, width), half
    )

    ga.ring_step(ga.one, first, 3, 2)
    go.ring_step(go.line, slab, 3, 1, False)
    ga.ring_step(ga.one, first, 3, 3)
    go.ring_step(go.line, slab, 3, 2, False)
    gh.ring_step(gh.line, every_h, 3, 1)
    ga.ring_step(ga.one, first, 3, 4)
    ga.column_begin(first, 17)
    go.ring_step(go.line, slab, 3, 3, False)
    ga.ring_step(ga.line, last, 10, 1)
    gh.ring_step(gh.line, every_h, 3, 2)
    go.ring_step(go.line, slab, 3, 4, False)
    go.y_begin(10)
    ga.ring_step(ga.line, last, 10, 2)
    gh.ring_step(gh.line, every_h, 3, 3)
    go.y_step(10, 1)
    ga.column_step(first, 17)
    ga.ring_step(ga.line, last, 10, 3)
    gh.ring_step(gh.line, every_h, 3, 4)
    go.y_step(10, 2)
    ga.column_end(first, 17)
    ga.ring_step(ga.line, last, 10, 4)
    ga.paired()

    before, after = (
        {"node": (node + NZ * NX - 1) % (NZ * NX)},
        {"node": (node + 1) % (NZ * NX)},
    )

    def halo(t, way):
        columns = lane(t * TILE, TILE)
        source, target_rows, peer = (
            (HALO, rows + HALO, before),
            (rows, 0, after),
        )[way]
        return pltpu.make_async_remote_copy(
            src_ref=kv.at[:, pl.ds(source, HALO), columns],
            dst_ref=kv.at[:, pl.ds(target_rows, HALO), columns],
            send_sem=halo_send.at[way, t],
            recv_sem=halo_recv.at[way, t],
            device_id=peer,
            device_id_type=MESH,
        )

    @pl.loop(0, width // TILE)
    def _(t):
        def product(base):
            columns = lane(base + t * TILE, TILE)
            return mat(normed[...], wqkv[:, :, :, columns].reshape(width, TILE))

        inner = pl.ds(HALO, rows)
        for base, unit, kept in ((0, q_unit, q_factor), (width, k_unit, k_factor)):
            full = product(base)
            for side in range(TILE // 128):
                part = full[:, side * 128 : side * 128 + 128]
                columns = lane(t * TILE + side * 128, 128)
                scale = lax.rsqrt(head_mean(part * part) + 1e-06)
                unit[:, columns] = part * scale
                kept[:, columns] = scale
                if base:
                    kv[0, inner, columns] = (part * scale).astype(half)
                else:
                    q_half[:, columns] = (part * scale).astype(half)
        kv[1, inner, lane(t * TILE, TILE)] = product(2 * width).astype(half)
        halo(t, 0).start()
        halo(t, 1).start()

    go.y_step(10, 3)

    @pl.loop(0, width // TILE)
    def _(t):
        halo(t, 0).wait()
        halo(t, 1).wait()

    @pl.loop(0, width // 128)
    def _(p):
        columns = lane(p * 128, 128)
        keys, held = kv[0, :, columns], kv[1, :, columns]
        mixed = []
        for side, query in enumerate(two_heads(q_half[:, columns])):
            raised = jnp.exp(mat_back(query, keys) * 0.125) * near[...]
            weight = raised / jnp.sum(raised, axis=1, keepdims=True)
            attention[2 * p + side] = weight
            mixed.append(mat(weight.astype(half), held))
        left[0, :, columns] = jnp.where(head_side(), mixed[0], mixed[1]).astype(half)

    twin = at(z, x, y, 1 - core)
    sender.start(left.at[0], left.at[1], recv_core.at[0], twin)
    go.y_step(10, 4)
    go.paired()
    gh.paired()

    @pl.loop(0, width // TILE)
    def _(t):
        columns = lane(t * TILE, TILE)
        product = mat(left[0], wo[:, :, :, columns].reshape(width, TILE))
        settled[:, columns] = (nodes[:, columns].astype(f32) + product).astype(half)

    error = mat(settled[...], wh[...].reshape(width, wh.shape[3])) - target[...]
    differ[...] = error
    differs[0] = error.astype(half)
    ens = y % 4
    for d in (1, 2, 3):
        peer = {"ens": (ens + d) % 4}
        sender.start(differs.at[0], differs.at[d], ens_recv.at[d - 1], peer)
    own_sign = soft_sign(error)
    paired = jnp.zeros_like(error)
    for d in (1, 2, 3):
        landed(differs.at[d], ens_recv.at[d - 1])
        paired = paired + soft_sign(error - differs[d].astype(f32))
    members = 4
    coefficient = fair_weight / (2 * members * (members - 1)) + (1 - fair_weight) / (
        2 * members * members
    )
    core_grad = own_sign / members - 2 * coefficient * paired
    grad_pred = (area[...] * core_grad).astype(half)

    @pl.loop(0, width // TILE)
    def _(t):
        block = wh[pl.ds(2 * t, 2)].reshape(TILE, wh.shape[3])
        gs[:, lane(t * TILE, TILE)] = mat_back(grad_pred, block).astype(half)

    wide = width // 2
    mine, other = lane(core * wide, wide), lane((1 - core) * wide, wide)
    sender.start(gs.at[:, other], right.at[1], recv_core.at[1], twin)
    right[0] = gs[:, mine]

    @pl.loop(0, width // TILE)
    def _(t):
        block = wo[pl.ds(2 * t, 2)].reshape(TILE, width)
        gm[:, lane(t * TILE, TILE)] = mat_back(gs[...], block).astype(half)

    landed(left.at[1], recv_core.at[0])
    landed(right.at[1], recv_core.at[1])
    tall = width // NZ

    @pl.loop(0, NZ)
    def _(block):
        columns = lane(block * tall, tall)
        total = mat_across(left[0, :, columns], right[0])
        total = total + mat_across(left[1, :, columns], right[1])
        parts[block] = total.astype(half).reshape(parts.shape[1:])

    for d in range(1, NX):
        sender.start(
            parts.at[:, (x + d) % NX],
            from_x.at[d - 1],
            recv_x.at[d - 1],
            at(z, (x + d) % NX, y, core),
        )

    for group in range(2):
        @pl.loop(group * 4, group * 4 + 4)
        def _(p):
            columns = lane(p * 128, 128)
            keys, held = kv[0, :, columns], kv[1, :, columns]
            grads = two_heads(gm[:, columns])
            queries = two_heads(q_half[:, columns])
            logits, halves_of, query_grad = [], [], []
            for side in range(2):
                weight = attention[2 * p + side]
                scores = mat_back(grads[side], held)
                mean = jnp.sum(weight * scores, axis=1, keepdims=True)
                logit = (weight * (scores - mean)).astype(half)
                logits.append(logit)
                halves_of.append(weight.astype(half))
                query_grad.append(mat(logit, keys))
            grad = jnp.where(head_side(), query_grad[0], query_grad[1]) * 0.125
            unit = q_unit[:, columns]
            gq[:, columns] = (
                q_factor[:, columns] * (grad - unit * head_mean(grad * unit))
            ).astype(half)
            key_grad = (
                mat_across(logits[0], queries[0]) + mat_across(logits[1], queries[1])
            ) * 0.125
            value_grad = mat_across(halves_of[0], grads[0]) + mat_across(
                halves_of[1], grads[1]
            )
            for k, (grad, kept) in enumerate(((key_grad, dk), (value_grad, dv))):
                kept[:, columns] = grad[HALO : HALO + rows]
                halo_out[0, k, :, columns] = grad[:HALO].astype(half)
                halo_out[1, k, :, columns] = grad[
                    HALO + rows : 2 * HALO + rows
                ].astype(half)

        columns = pl.ds(group * wide, wide)
        for way, peer in enumerate((before, after)):
            sender.start(
                halo_out.at[way, :, :, columns],
                halo_in.at[way, :, :, columns],
                back_recv.at[way, group],
                peer,
            )

    @pl.loop(0, width // TILE)
    def _(t):
        block = wqkv[pl.ds(2 * t, 2), :, :, pl.ds(0, width)].reshape(TILE, width)
        gn[:, lane(t * TILE, TILE)] = mat_back(gq[...], block)

    for d in range(1, NX):
        landed(from_x.at[d - 1], recv_x.at[d - 1])
    total = parts[:, x].astype(f32)
    for d in range(1, NX):
        total = total + from_x[d - 1].astype(f32)
    halves[...] = total.astype(half)
    for d in range(1, NZ):
        sender.start(
            halves.at[(z + d) % NZ],
            from_z.at[d - 1],
            recv_z.at[d - 1],
            at((z + d) % NZ, x, y, core),
        )

    for way in range(2):
        for group in range(2):
            region = halo_in.at[way, :, :, pl.ds(group * wide, wide)]
            landed(region, back_recv.at[way, group])
    for k, kept in enumerate((dk, dv)):
        low, high = pl.ds(0, HALO), pl.ds(rows - HALO, HALO)
        kept[low, :] = kept[low, :] + halo_in[1, k].astype(f32)
        kept[high, :] = kept[high, :] + halo_in[0, k].astype(f32)

    @pl.loop(0, width // 128)
    def _(p):
        columns = lane(p * 128, 128)
        grad, unit = dk[:, columns], k_unit[:, columns]
        gk[:, columns] = (
            k_factor[:, columns] * (grad - unit * head_mean(grad * unit))
        ).astype(half)
        gv[:, columns] = dv[:, columns].astype(half)

    @pl.loop(0, width // TILE)
    def _(t):
        columns = lane(t * TILE, TILE)
        blocks = wqkv.at[pl.ds(2 * t, 2)]
        keys = blocks[:, :, :, pl.ds(width, width)].reshape(TILE, width)
        held = blocks[:, :, :, pl.ds(2 * width, width)].reshape(TILE, width)
        gn[:, columns] = (
            gn[:, columns] + mat_back(gk[...], keys) + mat_back(gv[...], held)
        )

    @pl.loop(0, rows // 32)
    def _(t):
        block = pl.ds(pl.multiple_of(t * 32, 32), 32)
        grad, unit = gn[block, :], normal[block, :]
        centre = jnp.mean(grad, axis=1, keepdims=True)
        along = jnp.mean(grad * unit, axis=1, keepdims=True)
        change = factor[block, pl.ds(0, 1)] * (grad - centre - unit * along)
        out[block, :] = (gs[block, :].astype(f32) + change).astype(half)

    for d in range(1, NZ):
        landed(from_z.at[d - 1], recv_z.at[d - 1])
    total = halves[z].astype(f32)
    for d in range(1, NZ):
        total = total + from_z[d - 1].astype(f32)
    for k in range(pieces.shape[0]):
        pieces[k] = total[2 * k : 2 * k + 2, :]
    for dc in range(2):
        for dy in range(NY):
            if dy or dc:
                to_y, to_core = (y + dy) % NY, (core + dc) % 2
                index = (to_y % 4) * 4 + (to_y // 4) * 2 + to_core
                slot = dc * NY + dy
                sender.start(
                    pieces.at[index],
                    from_y.at[slot],
                    recv_y.at[slot],
                    at(z, x, to_y, to_core),
                )
    for dc in range(2):
        total = jnp.zeros(pieces.shape[1:], f32)
        for dy in range(NY):
            slot = dc * NY + dy
            if slot:
                landed(from_y.at[slot], recv_y.at[slot])
                total = total + from_y[slot]
            else:
                total = total + pieces[(y % 4) * 4 + (y // 4) * 2 + core]
        out_sum[:, (mine, other)[dc]] = total
    sender.finish()


def shards(
    nodes, w_query, w_key, w_value, w_output, w_head, neighbours, edge_counts, target, node_area
):
    rows, width = nodes.shape[2:]
    variables = w_head.shape[1]
    wide, block = width // 2, width // NZ // NX
    own = width // (NZ * NX * 2 * NY)
    f32, half = jnp.float32, jnp.bfloat16

    def vmem(shape, kind=half):
        return pltpu.VMEM(shape, kind)

    full = (rows, width)
    dma = pltpu.SemaphoreType.DMA
    scratch = [
        vmem((NZ, NX, block, 3 * width)),
        vmem((NZ, NX, block, width)),
        vmem((NZ, NX, block, variables)),
        vmem(full, f32),
        vmem(full),
        vmem((rows, 128), f32),
        vmem(full, f32),
        vmem(full, f32),
        vmem(full, f32),
        vmem(full, f32),
        vmem(full),
        vmem((2, EXT, width)),
        vmem((rows, EXT), f32),
        vmem((HEADS, rows, EXT), f32),
        vmem((2, rows, width)),
        vmem((2, rows, wide)),
        vmem(full),
        vmem((rows, variables), f32),
        vmem((4, rows, variables)),
        vmem(full),
        vmem(full),
        vmem(full),
        vmem(full, f32),
        vmem(full, f32),
        vmem(full),
        vmem(full),
        vmem(full, f32),
        vmem((2, 2, HALO, width)),
        vmem((2, 2, HALO, width)),
        vmem((NZ, NX, block, wide)),
        vmem((NX - 1, NZ, block, wide)),
        vmem((NZ, block, wide)),
        vmem((NZ - 1, block, wide)),
        vmem((2 * NY, own, wide), f32),
        vmem((2 * NY, own, wide), f32),
        dma((5,)),
        dma((160,)),
        dma((21,)),
        dma((17,)),
        dma((10,)),
        dma((3,)),
        dma((2, width // TILE)),
        dma((2, width // TILE)),
        dma((2, 2)),
        dma((3,)),
        dma((2,)),
        dma((NX - 1,)),
        dma((NZ - 1,)),
        dma((2 * NY,)),
    ]
    inside = pl.BlockSpec(memory_space=pltpu.VMEM)
    outside = pl.BlockSpec(memory_space=pl.ANY)
    grad_nodes, grad_out_proj = pl.pallas_call(
        layer_kernel,
        out_shape=[
            jax.ShapeDtypeStruct(full, half),
            jax.ShapeDtypeStruct((own, width), f32),
        ],
        in_specs=[inside] + [outside] * 5 + [inside] * 4,
        out_specs=[inside, inside],
        scratch_shapes=scratch,
        compiler_params=pltpu.CompilerParams(
            collective_id=0, has_side_effects=True, vmem_limit_bytes=48 * 2**20
        ),
        name="layer",
    )(
        nodes.reshape(full),
        w_query,
        w_key,
        w_value,
        w_output,
        w_head,
        neighbours,
        edge_counts.reshape(rows, 1),
        target.reshape(rows, variables),
        node_area.reshape(rows, 1),
    )
    return grad_nodes.reshape(nodes.shape), grad_out_proj.reshape(-1)


def solution(mesh):
    placed = (
        P("dp", "ens", "node", None),
        P("node", None),
        P("node", None),
        P("node", None),
        P("node", None),
        P("node", None),
        P("node", None),
        P("node"),
        P("dp", "node", None),
        P("node"),
    )
    return jax.shard_map(
        shards,
        mesh=mesh,
        in_specs=placed,
        out_specs=(P("dp", "ens", "node", None), P(("node", "ens", "dp"))),
        check_vma=False,
    )
```

```python
import jax
import jax.numpy as jnp
from jax import lax
from jax.experimental import pallas as pl
from jax.experimental.pallas import tpu as pltpu
from jax.sharding import PartitionSpec as P

HEADS = 16


fair_weight = 0.95
soft_square = 0.25

NZ, NX, NY = 8, 4, 8
MESH = pl.DeviceIdType.MESH


def place():
    node = lax.axis_index("node")
    ens = lax.axis_index("ens")
    dp = lax.axis_index("dp")
    return node // NX, node % NX, (dp // 2) * 4 + ens, dp % 2


def at(z, x, y, core):
    return {"node": z * NX + x, "ens": y % 4, "dp": (y // 4) * 2 + core}


class Sender:
    def __init__(self, sems, first=0):
        self.sems, self.count, self.sent = sems, first, []

    def start(self, src, dst, recv_sem, device):
        copy = pltpu.make_async_remote_copy(
            src_ref=src,
            dst_ref=dst,
            send_sem=self.sems.at[self.count],
            recv_sem=recv_sem,
            device_id=device,
            device_id_type=MESH,
        )
        self.count += 1
        copy.start()
        self.sent.append(copy)

    def finish(self):
        for copy in self.sent:
            copy.wait_send()
        self.sent = []


def landed(region, sem):
    pltpu.make_async_copy(region, region, sem).wait()


def greet(peers):
    barrier = pltpu.get_barrier_semaphore()
    for peer in peers:
        pl.semaphore_signal(barrier, inc=1, device_id=peer, device_id_type=MESH)
    pl.semaphore_wait(barrier, len(peers))


TILE = 256
HALO = 32
EXT = 256
FIRST = 2048
BY_X = 384
SENDS = 130
ORDER = (0, -1, 1, -2, 2, -3, 3, 4)


def spread(z):
    return (z + 2 * NZ) % NZ


class Gather:
    def __init__(self, whole, rows, columns, sender, recv, pair):
        self.whole, self.rows, self.columns = whole, rows, columns
        self.sender, self.recv, self.pair = sender, recv, pair
        z, x, y, core = place()
        self.z, self.x, self.y, self.core = z, x, y, core
        self.near = [at(z, (x + d) % NX, y, core) for d in (1, 2, 3)]
        self.up = at((z + 1) % NZ, x, y, core)
        self.down = at((z + NZ - 1) % NZ, x, y, core)
        self.twin = at(z, x, y, 1 - core)

    def send(self, region, sem, peer):
        self.sender.start(region, region, self.recv.at[sem], peer)

    def landed(self, region, sem):
        landed(region, self.recv.at[sem])

    def share(self, region):
        self.sender.start(region, region, self.pair, self.twin)

    def block(self, dz, dx, columns=None):
        z, x = spread(self.z + dz), (self.x + dx + NX) % NX
        return self.whole.at[z, x, self.rows, columns or self.columns]

    def line(self, dz, columns=None):
        return self.whole.at[
            spread(self.z + dz), :, self.rows, columns or self.columns
        ]


    def across(self, base=0):
        for d in range(3):
            self.send(self.block(0, 0), base + d, self.near[d])

    def crossed(self, base=0):
        for d in (1, 2, 3):
            self.landed(self.block(0, -d), base + d - 1)

    def ring_begin(self, columns, base):
        self.send(self.line(0, columns), base, self.up)
        self.send(self.line(0, columns), base + 4, self.down)

    def ring_step(self, columns, base, s):
        low, high = self.line(-s, columns), self.line(s, columns)
        self.landed(low, base + s - 1)
        if s < 4:
            self.send(low, base + s, self.up)
            self.landed(high, base + s + 3)
            if s < 3:
                self.send(high, base + s + 4, self.down)
        self.share(low)
        if s < 4:
            self.share(high)


    def fan(self, index):
        region = self.block(ORDER[index], 0)
        self.send(region, 7 + index, self.near[0])
        self.send(region, 15 + index, self.near[2])

    def column_begin(self):
        self.send(self.block(0, 0), 0, self.up)
        self.send(self.block(0, 0), 4, self.down)
        self.fan(0)

    def column_step(self, s):
        low, high = self.block(-s, 0), self.block(s, 0)
        self.landed(low, s - 1)
        if s < 4:
            self.send(low, s, self.up)
        self.fan(ORDER.index(-s if s < 4 else 4))
        if s < 4:
            self.landed(high, s + 3)
            if s < 3:
                self.send(high, s + 4, self.down)
            self.fan(ORDER.index(s))
        self.share(low)
        if s < 4:
            self.share(high)

    def column_pass(self, index):
        for dx, base, onward in ((-1, 7, self.near[0]), (1, 15, self.near[2])):
            region = self.block(ORDER[index], dx)
            self.landed(region, base + index)
            if (index % 2 == 0) == (dx < 0):
                self.send(region, 23 + index, onward)
            self.share(region)

    def column_end(self, index):
        region = self.block(ORDER[index], 2)
        self.landed(region, 23 + index)
        self.share(region)


    def plane(self):
        z, x, y, core = self.z, self.x, self.y, self.core
        for d in range(1, NZ):
            self.send(self.line(0), 2 + d, at((z + d) % NZ, x, y, core))

    def planed(self):
        for d in range(1, NZ):
            self.landed(self.line(-d), 2 + d)


    def slab(self, dy):
        width = self.whole.shape[3] // NY
        first = pl.multiple_of(((self.y + dy + NY) % NY) * width, width)
        return self.whole.at[:, :, self.rows, pl.ds(first, width)]

    def y_begin(self, base=10):
        z, x, y, core = self.z, self.x, self.y, self.core
        self.send(self.slab(0), base, at(z, x, (y + 1) % NY, core))
        self.send(self.slab(0), base + 4, at(z, x, (y + NY - 1) % NY, core))
        self.share(self.slab(0))

    def y_step(self, s, base=10):
        z, x, y, core = self.z, self.x, self.y, self.core
        low, high = self.slab(-s), self.slab(s)
        self.landed(low, base + s - 1)
        if s < 4:
            self.send(low, base + s, at(z, x, (y + 1) % NY, core))
            self.landed(high, base + s + 3)
            if s < 3:
                self.send(high, base + s + 4, at(z, x, (y + NY - 1) % NY, core))
        self.share(low)
        if s < 4:
            self.share(high)


def all_peers():
    z, x, y, core = place()
    node = z * NX + x
    peers = [at(z, (x + d) % NX, y, core) for d in range(1, NX)]
    peers += [at((z + d) % NZ, x, y, core) for d in range(1, NZ)]
    for dy in range(NY):
        for dc in range(2):
            if dy or dc:
                peers.append(at(z, x, (y + dy) % NY, (core + dc) % 2))
    peers.append({"node": (node + 1) % (NZ * NX)})
    peers.append({"node": (node + NZ * NX - 1) % (NZ * NX)})
    return peers


def mat(left, right):
    return jnp.dot(left, right, preferred_element_type=jnp.float32)


def mat_back(left, right):
    return lax.dot_general(
        left, right, (((1,), (1,)), ((), ())), preferred_element_type=jnp.float32
    )


def mat_across(left, right):
    return lax.dot_general(
        left, right, (((0,), (0,)), ((), ())), preferred_element_type=jnp.float32
    )


def soft_sign(values):
    return values * lax.rsqrt(values * values + soft_square)


def lane(start, size):
    return pl.ds(pl.multiple_of(start, size), size)


def head_side():
    return lax.broadcasted_iota(jnp.int32, (1, 128), 1) < 64


def head_mean(values):
    side = head_side()
    low = jnp.sum(jnp.where(side, values, 0.0), axis=1, keepdims=True)
    high = jnp.sum(jnp.where(side, 0.0, values), axis=1, keepdims=True)
    return jnp.where(side, low, high) * (1.0 / 64)


def two_heads(values):
    side = head_side()
    empty = jnp.zeros_like(values)
    return jnp.where(side, values, empty), jnp.where(side, empty, values)


def layer_kernel(
    nodes_in, wq_shard, wk_shard, wv_shard, wo_shard, wh_shard, neighbours_in,
    counts_in, target_in, area_in, out, out_sum,
    nodes, neighbours, counts, target, area,
    wqkv, wo, wh, normal, normed, factor, q_unit, k_unit, q_factor, k_factor, q_half,
    kv, near, attention, left, right, settled, differ, differs, gs, gm, gq, dk, dv,
    gk, gv, gn, halo_out, halo_in, parts, from_x, halves, from_z, parts_b, from_z_b,
    halves_b, from_x_b, pieces, from_y,
    local, send, recv_a, recv_o, recv_h, pair, halo_send, halo_recv, back_recv,
    ens_recv, recv_core, recv_x, recv_z, recv_x_b, recv_z_b, recv_y,
):
    f32, half = jnp.float32, jnp.bfloat16
    z, x, y, core = place()
    node = z * NX + x
    rows, width = nodes.shape
    small = [
        pltpu.make_async_copy(source, kept, local.at[k])
        for k, (source, kept) in enumerate(
            (
                (nodes_in, nodes),
                (neighbours_in, neighbours),
                (counts_in, counts),
                (target_in, target),
                (area_in, area),
            )
        )
    ]
    own_half = pl.ds(pl.multiple_of(core * 16, 16), 16)
    slab = pl.ds(pl.multiple_of(y * 128, 128), 128)
    every = pl.ds(0, width)
    every_h = pl.ds(0, wh_shard.shape[1])

    def own(k, shard, whole, taken_rows, taken, kept):
        return pltpu.make_async_copy(
            shard.at[taken_rows, taken],
            whole.at[z, x, taken_rows, kept],
            local.at[5 + k],
        )

    all_rows = pl.ds(0, wq_shard.shape[0])
    own_o = own(0, wo_shard, wo, own_half, slab, slab)
    own_h = own(1, wh_shard, wh, own_half, every_h, every_h)

    def own_a(which):
        if which:
            kept = pl.ds(FIRST, width)
            return [own(2, wv_shard, wqkv, all_rows, every, kept)]
        return [
            own(2, wq_shard, wqkv, all_rows, every, pl.ds(0, width)),
            own(3, wk_shard, wqkv, all_rows, every, pl.ds(width, width)),
        ]

    def normalise():
        small[0].wait()
        values = nodes[...].astype(f32)
        shifted = values - jnp.mean(values, axis=1, keepdims=True)
        scale = lax.rsqrt(jnp.mean(shifted * shifted, axis=1, keepdims=True) + 1e-05)
        factor[...] = jnp.broadcast_to(scale, factor.shape)
        normal[...] = shifted * scale
        normed[...] = normal[...].astype(half)

    def find_near():
        small[1].wait()
        small[2].wait()
        total = NZ * NX * rows
        column = (neighbours[...] - node * rows + HALO + total) & (total - 1)
        at_column = lax.broadcasted_iota(jnp.int32, (EXT, rows), 0)
        hits = jnp.zeros((EXT, rows), f32)
        for s in range(neighbours.shape[0]):
            hit = (column[s : s + 1, :] == at_column) & (counts[...] > s)
            hits = hits + jnp.where(hit, 1.0, 0.0)
        near[...] = hits.T
        kv[:, pl.ds(rows + 2 * HALO, EXT - rows - 2 * HALO)] = jnp.zeros(
            (2, EXT - rows - 2 * HALO, width), half
        )

    def gather(which):
        sender = Sender(send)
        columns = (pl.ds(0, FIRST), pl.ds(FIRST, 3 * width - FIRST))
        ga = Gather(wqkv, all_rows, columns[which], sender, recv_a, pair.at[0])
        go = Gather(wo, own_half, slab, sender, recv_o, pair.at[1])
        gh = Gather(wh, own_half, every_h, sender, recv_h, pair.at[2])
        for load in own_a(which):
            load.wait()
        if which:
            ga.across()
        else:
            ga.column_begin()
        own_o.wait()
        go.across()
        own_h.wait()
        gh.across()
        ga.share(ga.block(0, 0))
        normalise()
        if which:
            chunk = (3 * width - FIRST) // 2
            chunks = [(pl.ds(FIRST + k * chunk, chunk), 3 + 7 * k) for k in range(2)]
            ga.crossed()
            for part in chunks:
                ga.ring_begin(*part)
            go.crossed()
            go.plane()
            for d in (1, 2, 3):
                ga.share(ga.block(0, -d))
            find_near()
            for s in (1, 2, 3, 4):
                for part in chunks:
                    ga.ring_step(*part, s)
                if s == 1:
                    go.planed()
                    go.y_begin()
                if s == 3:
                    go.y_step(1)
                    gh.crossed()
                    gh.plane()
            go.y_step(2)
        else:
            ga.column_step(1)
            go.crossed()
            go.plane()
            ga.column_pass(0)
            ga.column_step(2)
            find_near()
            ga.column_pass(1)
            go.planed()
            go.y_begin()
            ga.column_step(3)
            ga.column_pass(2)
            ga.column_step(4)
            ga.column_pass(3)
            gh.crossed()
            gh.plane()
            ga.column_pass(4)
            ga.column_end(0)
            go.y_step(1)
            ga.column_pass(5)
            ga.column_end(1)
            ga.column_pass(6)
            ga.column_end(2)
            ga.column_pass(7)
            for index in (3, 4, 5, 6, 7):
                ga.column_end(index)
            go.y_step(2)
        landed(wqkv.at[:, :, :, columns[1 - which]], pair.at[0])
        sender.finish()

    for which in range(2):
        @pl.when(core == which)
        def _():
            for load in own_a(which):
                load.start()

    own_o.start()
    own_h.start()
    for load in small:
        load.start()
    greet(all_peers())
    for which in range(2):
        @pl.when(core == which)
        def _():
            gather(which)

    sender = Sender(send, SENDS)
    go = Gather(wo, own_half, slab, sender, recv_o, pair.at[1])
    gh = Gather(wh, own_half, every_h, sender, recv_h, pair.at[2])

    before, after = (
        {"node": (node + NZ * NX - 1) % (NZ * NX)},
        {"node": (node + 1) % (NZ * NX)},
    )

    def halo(t, way):
        columns = lane(t * TILE, TILE)
        source, target_rows, peer = (
            (HALO, rows + HALO, before),
            (rows, 0, after),
        )[way]
        return pltpu.make_async_remote_copy(
            src_ref=kv.at[:, pl.ds(source, HALO), columns],
            dst_ref=kv.at[:, pl.ds(target_rows, HALO), columns],
            send_sem=halo_send.at[way, t],
            recv_sem=halo_recv.at[way, t],
            device_id=peer,
            device_id_type=MESH,
        )

    @pl.loop(0, width // TILE)
    def _(t):
        def product(base):
            columns = lane(base + t * TILE, TILE)
            return mat(normed[...], wqkv[:, :, :, columns].reshape(width, TILE))

        inner = pl.ds(HALO, rows)
        for base, unit, kept in ((0, q_unit, q_factor), (width, k_unit, k_factor)):
            full = product(base)
            for side in range(TILE // 128):
                part = full[:, side * 128 : side * 128 + 128]
                columns = lane(t * TILE + side * 128, 128)
                scale = lax.rsqrt(head_mean(part * part) + 1e-06)
                unit[:, columns] = part * scale
                kept[:, columns] = scale
                if base:
                    kv[0, inner, columns] = (part * scale).astype(half)
                else:
                    q_half[:, columns] = (part * scale).astype(half)
        kv[1, inner, lane(t * TILE, TILE)] = product(2 * width).astype(half)
        halo(t, 0).start()
        halo(t, 1).start()

    go.y_step(3)
    gh.planed()
    gh.share(wh.at[:, :, own_half])

    @pl.loop(0, width // TILE)
    def _(t):
        halo(t, 0).wait()
        halo(t, 1).wait()

    @pl.loop(0, width // 128)
    def _(p):
        columns = lane(p * 128, 128)
        keys, held = kv[0, :, columns], kv[1, :, columns]
        mixed = []
        for side, query in enumerate(two_heads(q_half[:, columns])):
            raised = jnp.exp(mat_back(query, keys) * 0.125) * near[...]
            weight = raised / jnp.sum(raised, axis=1, keepdims=True)
            attention[2 * p + side] = weight
            mixed.append(mat(weight.astype(half), held))
        left[0, :, columns] = jnp.where(head_side(), mixed[0], mixed[1]).astype(half)

    twin = at(z, x, y, 1 - core)
    sender.start(left.at[0], left.at[1], recv_core.at[0], twin)
    go.y_step(4)
    landed(wo.at[:, :, pl.ds(0, 16)], pair.at[1])
    landed(wh.at[:, :, pl.ds(0, 16)], pair.at[2])
    small[3].wait()
    small[4].wait()

    @pl.loop(0, width // TILE)
    def _(t):
        columns = lane(t * TILE, TILE)
        product = mat(left[0], wo[:, :, :, columns].reshape(width, TILE))
        settled[:, columns] = (nodes[:, columns].astype(f32) + product).astype(half)

    error = mat(settled[...], wh[...].reshape(width, wh.shape[3])) - target[...]
    differ[...] = error
    differs[0] = error.astype(half)
    ens = y % 4
    for d in (1, 2, 3):
        peer = {"ens": (ens + d) % 4}
        sender.start(differs.at[0], differs.at[d], ens_recv.at[d - 1], peer)
    own_sign = soft_sign(error)
    paired = jnp.zeros_like(error)
    for d in (1, 2, 3):
        landed(differs.at[d], ens_recv.at[d - 1])
        paired = paired + soft_sign(error - differs[d].astype(f32))
    members = 4
    coefficient = fair_weight / (2 * members * (members - 1)) + (1 - fair_weight) / (
        2 * members * members
    )
    core_grad = own_sign / members - 2 * coefficient * paired
    weight = jnp.broadcast_to(area[...], (rows, rows)).T
    grad_pred = (weight * core_grad).astype(half)

    @pl.loop(0, width // TILE)
    def _(t):
        block = wh[pl.ds(2 * t, 2)].reshape(TILE, wh.shape[3])
        gs[:, lane(t * TILE, TILE)] = mat_back(grad_pred, block).astype(half)

    wide = width // 2
    mine, other = lane(core * wide, wide), lane((1 - core) * wide, wide)
    sender.start(gs.at[:, other], right.at[1], recv_core.at[1], twin)
    right[0] = gs[:, mine]

    @pl.loop(0, width // TILE)
    def _(t):
        block = wo[pl.ds(2 * t, 2)].reshape(TILE, width)
        gm[:, lane(t * TILE, TILE)] = mat_back(gs[...], block).astype(half)

    landed(left.at[1], recv_core.at[0])
    landed(right.at[1], recv_core.at[1])
    tall = width // NZ

    @pl.loop(0, NZ)
    def _(block):
        columns = lane(block * tall, tall)
        total = mat_across(left[0, :, columns], right[0])
        total = total + mat_across(left[1, :, columns], right[1])
        parts[block] = total[:, :BY_X].astype(half).reshape(parts.shape[1:])
        parts_b[block] = total[:, BY_X:].astype(half).reshape(parts_b.shape[1:])

    for d in range(1, NX):
        sender.start(
            parts.at[:, (x + d) % NX],
            from_x.at[d - 1],
            recv_x.at[d - 1],
            at(z, (x + d) % NX, y, core),
        )
    for d in range(1, NZ):
        sender.start(
            parts_b.at[(z + d) % NZ],
            from_z_b.at[d - 1],
            recv_z_b.at[d - 1],
            at((z + d) % NZ, x, y, core),
        )

    for group in range(2):
        @pl.loop(group * 4, group * 4 + 4)
        def _(p):
            columns = lane(p * 128, 128)
            keys, held = kv[0, :, columns], kv[1, :, columns]
            grads = two_heads(gm[:, columns])
            queries = two_heads(q_half[:, columns])
            logits, halves_of, query_grad = [], [], []
            for side in range(2):
                weight = attention[2 * p + side]
                scores = mat_back(grads[side], held)
                mean = jnp.sum(weight * scores, axis=1, keepdims=True)
                logit = (weight * (scores - mean)).astype(half)
                logits.append(logit)
                halves_of.append(weight.astype(half))
                query_grad.append(mat(logit, keys))
            grad = jnp.where(head_side(), query_grad[0], query_grad[1]) * 0.125
            unit = q_unit[:, columns]
            gq[:, columns] = (
                q_factor[:, columns] * (grad - unit * head_mean(grad * unit))
            ).astype(half)
            key_grad = (
                mat_across(logits[0], queries[0]) + mat_across(logits[1], queries[1])
            ) * 0.125
            value_grad = mat_across(halves_of[0], grads[0]) + mat_across(
                halves_of[1], grads[1]
            )
            for k, (grad, kept) in enumerate(((key_grad, dk), (value_grad, dv))):
                kept[:, columns] = grad[HALO : HALO + rows]
                halo_out[0, k, :, columns] = grad[:HALO].astype(half)
                halo_out[1, k, :, columns] = grad[
                    HALO + rows : 2 * HALO + rows
                ].astype(half)

        columns = pl.ds(group * wide, wide)
        for way, peer in enumerate((before, after)):
            sender.start(
                halo_out.at[way, :, :, columns],
                halo_in.at[way, :, :, columns],
                back_recv.at[way, group],
                peer,
            )

    @pl.loop(0, width // TILE)
    def _(t):
        block = wqkv[pl.ds(2 * t, 2), :, :, pl.ds(0, width)].reshape(TILE, width)
        gn[:, lane(t * TILE, TILE)] = mat_back(gq[...], block)

    for d in range(1, NX):
        landed(from_x.at[d - 1], recv_x.at[d - 1])
    total = parts[:, x].astype(f32)
    for d in range(1, NX):
        total = total + from_x[d - 1].astype(f32)
    halves[...] = total.astype(half)
    for d in range(1, NZ):
        sender.start(
            halves.at[(z + d) % NZ],
            from_z.at[d - 1],
            recv_z.at[d - 1],
            at((z + d) % NZ, x, y, core),
        )
    for d in range(1, NZ):
        landed(from_z_b.at[d - 1], recv_z_b.at[d - 1])
    total = parts_b[z].astype(f32)
    for d in range(1, NZ):
        total = total + from_z_b[d - 1].astype(f32)
    halves_b[...] = total.astype(half)
    for d in range(1, NX):
        sender.start(
            halves_b.at[(x + d) % NX],
            from_x_b.at[d - 1],
            recv_x_b.at[d - 1],
            at(z, (x + d) % NX, y, core),
        )

    for way in range(2):
        for group in range(2):
            region = halo_in.at[way, :, :, pl.ds(group * wide, wide)]
            landed(region, back_recv.at[way, group])
    for k, kept in enumerate((dk, dv)):
        low, high = pl.ds(0, HALO), pl.ds(rows - HALO, HALO)
        kept[low, :] = kept[low, :] + halo_in[1, k].astype(f32)
        kept[high, :] = kept[high, :] + halo_in[0, k].astype(f32)

    @pl.loop(0, width // 128)
    def _(p):
        columns = lane(p * 128, 128)
        grad, unit = dk[:, columns], k_unit[:, columns]
        gk[:, columns] = (
            k_factor[:, columns] * (grad - unit * head_mean(grad * unit))
        ).astype(half)
        gv[:, columns] = dv[:, columns].astype(half)

    @pl.loop(0, width // TILE)
    def _(t):
        columns = lane(t * TILE, TILE)
        blocks = wqkv.at[pl.ds(2 * t, 2)]
        keys = blocks[:, :, :, pl.ds(width, width)].reshape(TILE, width)
        held = blocks[:, :, :, pl.ds(2 * width, width)].reshape(TILE, width)
        gn[:, columns] = (
            gn[:, columns] + mat_back(gk[...], keys) + mat_back(gv[...], held)
        )

    @pl.loop(0, rows // 32)
    def _(t):
        block = pl.ds(pl.multiple_of(t * 32, 32), 32)
        grad, unit = gn[block, :], normal[block, :]
        centre = jnp.mean(grad, axis=1, keepdims=True)
        along = jnp.mean(grad * unit, axis=1, keepdims=True)
        change = factor[block, pl.ds(0, 1)] * (grad - centre - unit * along)
        out[block, :] = (gs[block, :].astype(f32) + change).astype(half)

    for d in range(1, NZ):
        landed(from_z.at[d - 1], recv_z.at[d - 1])
    total = halves[z].astype(f32)
    for d in range(1, NZ):
        total = total + from_z[d - 1].astype(f32)
    for d in range(1, NX):
        landed(from_x_b.at[d - 1], recv_x_b.at[d - 1])
    total_b = halves_b[x].astype(f32)
    for d in range(1, NX):
        total_b = total_b + from_x_b[d - 1].astype(f32)
    for k in range(pieces.shape[0]):
        pieces[k, :, :BY_X] = total[2 * k : 2 * k + 2, :]
        pieces[k, :, BY_X:] = total_b[2 * k : 2 * k + 2, :]
    for dc in range(2):
        for dy in range(NY):
            if dy or dc:
                to_y, to_core = (y + dy) % NY, (core + dc) % 2
                index = (to_y % 4) * 4 + (to_y // 4) * 2 + to_core
                slot = dc * NY + dy
                sender.start(
                    pieces.at[index],
                    from_y.at[slot],
                    recv_y.at[slot],
                    at(z, x, to_y, to_core),
                )
    for dc in range(2):
        total = jnp.zeros(pieces.shape[1:], f32)
        for dy in range(NY):
            slot = dc * NY + dy
            if slot:
                landed(from_y.at[slot], recv_y.at[slot])
                total = total + from_y[slot]
            else:
                total = total + pieces[(y % 4) * 4 + (y // 4) * 2 + core]
        per = wide // 128
        for i in range(total.shape[0]):
            for j in range(per):
                first = i * NY + (core + dc) % 2 * per + j
                out_sum[pl.ds(first, 1), :] = total[i : i + 1, j * 128 : j * 128 + 128]
    sender.finish()


def shards(
    nodes, w_query, w_key, w_value, w_output, w_head, neighbours, edge_counts, target, node_area
):
    rows, width = nodes.shape[2:]
    variables = w_head.shape[1]
    wide, block = width // 2, width // NZ // NX
    own = width // (NZ * NX * 2 * NY)
    f32, half = jnp.float32, jnp.bfloat16

    def vmem(shape, kind=half):
        return pltpu.VMEM(shape, kind)

    full = (rows, width)
    dma = pltpu.SemaphoreType.DMA
    scratch = [
        vmem(full),
        vmem((neighbours.shape[1], rows), jnp.int32),
        vmem((1, rows), jnp.int32),
        vmem((rows, variables), f32),
        vmem((1, rows), f32),
        vmem((NZ, NX, block, 3 * width)),
        vmem((NZ, NX, block, width)),
        vmem((NZ, NX, block, variables)),
        vmem(full, f32),
        vmem(full),
        vmem((rows, 128), f32),
        vmem(full, f32),
        vmem(full, f32),
        vmem(full, f32),
        vmem(full, f32),
        vmem(full),
        vmem((2, EXT, width)),
        vmem((rows, EXT), f32),
        vmem((HEADS, rows, EXT), f32),
        vmem((2, rows, width)),
        vmem((2, rows, wide)),
        vmem(full),
        vmem((rows, variables), f32),
        vmem((4, rows, variables)),
        vmem(full),
        vmem(full),
        vmem(full),
        vmem(full, f32),
        vmem(full, f32),
        vmem(full),
        vmem(full),
        vmem(full, f32),
        vmem((2, 2, HALO, width)),
        vmem((2, 2, HALO, width)),
        vmem((NZ, NX, block, BY_X)),
        vmem((NX - 1, NZ, block, BY_X)),
        vmem((NZ, block, BY_X)),
        vmem((NZ - 1, block, BY_X)),
        vmem((NZ, NX, block, wide - BY_X)),
        vmem((NZ - 1, NX, block, wide - BY_X)),
        vmem((NX, block, wide - BY_X)),
        vmem((NX - 1, block, wide - BY_X)),
        vmem((2 * NY, own, wide), f32),
        vmem((2 * NY, own, wide), f32),
        dma((9,)),
        dma((SENDS + 64,)),
        dma((31,)),
        dma((17,)),
        dma((10,)),
        dma((3,)),
        dma((2, width // TILE)),
        dma((2, width // TILE)),
        dma((2, 2)),
        dma((3,)),
        dma((2,)),
        dma((NX - 1,)),
        dma((NZ - 1,)),
        dma((NX - 1,)),
        dma((NZ - 1,)),
        dma((2 * NY,)),
    ]
    inside = pl.BlockSpec(memory_space=pltpu.VMEM)
    outside = pl.BlockSpec(memory_space=pltpu.HBM)
    grad_nodes, grad_out_proj = pl.pallas_call(
        layer_kernel,
        out_shape=[
            jax.ShapeDtypeStruct(full, half),
            jax.ShapeDtypeStruct((own * NY, width // NY), f32),
        ],
        in_specs=[outside] * 10,
        out_specs=[inside, inside],
        scratch_shapes=scratch,
        compiler_params=pltpu.CompilerParams(
            collective_id=0, has_side_effects=True, vmem_limit_bytes=62 * 2**20
        ),
        name="layer",
    )(
        nodes.reshape(full),
        w_query,
        w_key,
        w_value,
        w_output,
        w_head,
        neighbours.T,
        edge_counts.reshape(1, rows),
        target.reshape(rows, variables),
        node_area.reshape(1, rows),
    )
    return grad_nodes.reshape(nodes.shape), grad_out_proj.reshape(-1)


def solution(mesh):
    placed = (
        P("dp", "ens", "node", None),
        P("node", None),
        P("node", None),
        P("node", None),
        P("node", None),
        P("node", None),
        P("node", None),
        P("node"),
        P("dp", "node", None),
        P("node"),
    )
    return jax.shard_map(
        shards,
        mesh=mesh,
        in_specs=placed,
        out_specs=(P("dp", "ens", "node", None), P(("node", "ens", "dp"))),
        check_vma=False,
    )
```

```python
import jax
import jax.numpy as jnp
from jax import lax
from jax.experimental import pallas as pl
from jax.experimental.pallas import tpu as pltpu
from jax.sharding import PartitionSpec as P

HEADS = 16


fair_weight = 0.95
soft_square = 0.25

NZ, NX, NY = 8, 4, 8
MESH = pl.DeviceIdType.MESH


def place():
    node = lax.axis_index("node")
    ens = lax.axis_index("ens")
    dp = lax.axis_index("dp")
    return node // NX, node % NX, (dp // 2) * 4 + ens, dp % 2


def at(z, x, y, core):
    return {"node": z * NX + x, "ens": y % 4, "dp": (y // 4) * 2 + core}


class Sender:
    def __init__(self, sems, first=0):
        self.sems, self.count, self.sent = sems, first, []

    def start(self, src, dst, recv_sem, device):
        copy = pltpu.make_async_remote_copy(
            src_ref=src,
            dst_ref=dst,
            send_sem=self.sems.at[self.count],
            recv_sem=recv_sem,
            device_id=device,
            device_id_type=MESH,
        )
        self.count += 1
        copy.start()
        self.sent.append(copy)

    def finish(self):
        for copy in self.sent:
            copy.wait_send()
        self.sent = []


def landed(region, sem):
    pltpu.make_async_copy(region, region, sem).wait()


def greet(peers):
    barrier = pltpu.get_barrier_semaphore()
    for peer in peers:
        pl.semaphore_signal(barrier, inc=1, device_id=peer, device_id_type=MESH)
    pl.semaphore_wait(barrier, len(peers))


TILE = 256
HALO = 32
EXT = 256
FIRST = 1792
BY_X = 384
SENDS = 130
ORDER = (0, -1, 1, -2, 2, -3, 3, 4)


def spread(z):
    return (z + 2 * NZ) % NZ


class Gather:
    def __init__(self, whole, rows, columns, sender, recv, pair):
        self.whole, self.rows, self.columns = whole, rows, columns
        self.sender, self.recv, self.pair = sender, recv, pair
        z, x, y, core = place()
        self.z, self.x, self.y, self.core = z, x, y, core
        self.near = [at(z, (x + d) % NX, y, core) for d in (1, 2, 3)]
        self.up = at((z + 1) % NZ, x, y, core)
        self.down = at((z + NZ - 1) % NZ, x, y, core)
        self.twin = at(z, x, y, 1 - core)

    def send(self, region, sem, peer):
        self.sender.start(region, region, self.recv.at[sem], peer)

    def landed(self, region, sem):
        landed(region, self.recv.at[sem])

    def share(self, region):
        self.sender.start(region, region, self.pair, self.twin)

    def block(self, dz, dx, columns=None):
        z, x = spread(self.z + dz), (self.x + dx + NX) % NX
        return self.whole.at[z, x, self.rows, columns or self.columns]

    def line(self, dz, columns=None):
        return self.whole.at[
            spread(self.z + dz), :, self.rows, columns or self.columns
        ]


    def across(self, base=0):
        for d in range(3):
            self.send(self.block(0, 0), base + d, self.near[d])

    def crossed(self, base=0):
        for d in (1, 2, 3):
            self.landed(self.block(0, -d), base + d - 1)

    def ring_begin(self, columns, base):
        self.send(self.line(0, columns), base, self.up)
        self.send(self.line(0, columns), base + 4, self.down)

    def ring_step(self, columns, base, s):
        low, high = self.line(-s, columns), self.line(s, columns)
        self.landed(low, base + s - 1)
        if s < 4:
            self.send(low, base + s, self.up)
            self.landed(high, base + s + 3)
            if s < 3:
                self.send(high, base + s + 4, self.down)
        self.share(low)
        if s < 4:
            self.share(high)


    def fan(self, index):
        region = self.block(ORDER[index], 0)
        self.send(region, 7 + index, self.near[0])
        self.send(region, 15 + index, self.near[2])

    def column_begin(self):
        self.send(self.block(0, 0), 0, self.up)
        self.send(self.block(0, 0), 4, self.down)
        self.fan(0)

    def column_step(self, s):
        low, high = self.block(-s, 0), self.block(s, 0)
        self.landed(low, s - 1)
        if s < 4:
            self.send(low, s, self.up)
        self.fan(ORDER.index(-s if s < 4 else 4))
        if s < 4:
            self.landed(high, s + 3)
            if s < 3:
                self.send(high, s + 4, self.down)
            self.fan(ORDER.index(s))
        self.share(low)
        if s < 4:
            self.share(high)

    def column_pass(self, index):
        for dx, base, onward in ((-1, 7, self.near[0]), (1, 15, self.near[2])):
            region = self.block(ORDER[index], dx)
            self.landed(region, base + index)
            if (index % 2 == 0) == (dx < 0):
                self.send(region, 23 + index, onward)
            self.share(region)

    def column_end(self, index):
        region = self.block(ORDER[index], 2)
        self.landed(region, 23 + index)
        self.share(region)


    def plane(self):
        z, x, y, core = self.z, self.x, self.y, self.core
        for d in range(1, NZ):
            self.send(self.line(0), 2 + d, at((z + d) % NZ, x, y, core))

    def planed(self):
        for d in range(1, NZ):
            self.landed(self.line(-d), 2 + d)


    def slab(self, dy):
        width = self.whole.shape[3] // NY
        first = pl.multiple_of(((self.y + dy + NY) % NY) * width, width)
        return self.whole.at[:, :, self.rows, pl.ds(first, width)]

    def y_begin(self, base=10):
        z, x, y, core = self.z, self.x, self.y, self.core
        self.send(self.slab(0), base, at(z, x, (y + 1) % NY, core))
        self.send(self.slab(0), base + 4, at(z, x, (y + NY - 1) % NY, core))
        self.share(self.slab(0))

    def y_step(self, s, base=10):
        z, x, y, core = self.z, self.x, self.y, self.core
        low, high = self.slab(-s), self.slab(s)
        self.landed(low, base + s - 1)
        if s < 4:
            self.send(low, base + s, at(z, x, (y + 1) % NY, core))
            self.landed(high, base + s + 3)
            if s < 3:
                self.send(high, base + s + 4, at(z, x, (y + NY - 1) % NY, core))
        self.share(low)
        if s < 4:
            self.share(high)


def all_peers():
    z, x, y, core = place()
    node = z * NX + x
    peers = [at(z, (x + d) % NX, y, core) for d in range(1, NX)]
    peers += [at((z + d) % NZ, x, y, core) for d in range(1, NZ)]
    for dy in range(NY):
        for dc in range(2):
            if dy or dc:
                peers.append(at(z, x, (y + dy) % NY, (core + dc) % 2))
    peers.append({"node": (node + 1) % (NZ * NX)})
    peers.append({"node": (node + NZ * NX - 1) % (NZ * NX)})
    return peers


def mat(left, right):
    return jnp.dot(left, right, preferred_element_type=jnp.float32)


def mat_back(left, right):
    return lax.dot_general(
        left, right, (((1,), (1,)), ((), ())), preferred_element_type=jnp.float32
    )


def mat_across(left, right):
    return lax.dot_general(
        left, right, (((0,), (0,)), ((), ())), preferred_element_type=jnp.float32
    )


def soft_sign(values):
    return values * lax.rsqrt(values * values + soft_square)


def lane(start, size):
    return pl.ds(pl.multiple_of(start, size), size)


def head_side():
    return lax.broadcasted_iota(jnp.int32, (1, 128), 1) < 64


def head_mean(values):
    side = head_side()
    low = jnp.sum(jnp.where(side, values, 0.0), axis=1, keepdims=True)
    high = jnp.sum(jnp.where(side, 0.0, values), axis=1, keepdims=True)
    return jnp.where(side, low, high) * (1.0 / 64)


def two_heads(values):
    side = head_side()
    empty = jnp.zeros_like(values)
    return jnp.where(side, values, empty), jnp.where(side, empty, values)


def layer_kernel(
    nodes_in, wq_shard, wk_shard, wv_shard, wo_shard, wh_shard, neighbours_in,
    counts_in, target_in, area_in, out, out_sum,
    nodes, neighbours, counts, target, area,
    wqkv, wo, wh, normal, normed, factor, q_unit, k_unit, q_factor, k_factor, q_half,
    kv, near, attention, left, right, settled, differ, differs, gs, gm, gq, dk, dv,
    gk, gv, gn, halo_out, halo_in, parts, from_x, halves, from_z, parts_b, from_z_b,
    halves_b, from_x_b, pieces, from_y,
    local, send, recv_a, recv_o, recv_h, pair, halo_send, halo_recv, back_recv,
    ens_recv, recv_core, send_x, recv_x, recv_z, recv_x_b, recv_z_b, recv_y,
):
    f32, half = jnp.float32, jnp.bfloat16
    z, x, y, core = place()
    node = z * NX + x
    rows, width = nodes.shape
    small = [
        pltpu.make_async_copy(source, kept, local.at[k])
        for k, (source, kept) in enumerate(
            (
                (nodes_in, nodes),
                (neighbours_in, neighbours),
                (counts_in, counts),
                (target_in, target),
                (area_in, area),
            )
        )
    ]
    own_half = pl.ds(pl.multiple_of(core * 16, 16), 16)
    slab = pl.ds(pl.multiple_of(y * 128, 128), 128)
    every = pl.ds(0, width)
    every_h = pl.ds(0, wh_shard.shape[1])

    def own(k, shard, whole, taken_rows, taken, kept):
        return pltpu.make_async_copy(
            shard.at[taken_rows, taken],
            whole.at[z, x, taken_rows, kept],
            local.at[5 + k],
        )

    all_rows = pl.ds(0, wq_shard.shape[0])
    own_o = own(0, wo_shard, wo, own_half, slab, slab)
    own_h = own(1, wh_shard, wh, own_half, every_h, every_h)

    def own_a(which):
        rest = FIRST - width
        if which:
            end, kept = pl.ds(rest, width - rest), pl.ds(FIRST, width - rest)
            loads = [own(2, wv_shard, wqkv, all_rows, every, pl.ds(2 * width, width))]
            if rest < width:
                loads.append(own(3, wk_shard, wqkv, all_rows, end, kept))
            return loads
        start = pl.ds(0, rest)
        return [
            own(2, wq_shard, wqkv, all_rows, every, pl.ds(0, width)),
            own(3, wk_shard, wqkv, all_rows, start, pl.ds(width, rest)),
        ]

    def normalise():
        small[0].wait()
        values = nodes[...].astype(f32)
        shifted = values - jnp.mean(values, axis=1, keepdims=True)
        scale = lax.rsqrt(jnp.mean(shifted * shifted, axis=1, keepdims=True) + 1e-05)
        factor[...] = jnp.broadcast_to(scale, factor.shape)
        normal[...] = shifted * scale
        normed[...] = normal[...].astype(half)

    def find_near():
        small[1].wait()
        small[2].wait()
        total = NZ * NX * rows
        column = (neighbours[...] - node * rows + HALO + total) & (total - 1)
        at_column = lax.broadcasted_iota(jnp.int32, (EXT, rows), 0)
        hits = jnp.zeros((EXT, rows), f32)
        for s in range(neighbours.shape[0]):
            hit = (column[s : s + 1, :] == at_column) & (counts[...] > s)
            hits = hits + jnp.where(hit, 1.0, 0.0)
        near[...] = hits.T
        kv[:, pl.ds(rows + 2 * HALO, EXT - rows - 2 * HALO)] = jnp.zeros(
            (2, EXT - rows - 2 * HALO, width), half
        )

    def gather(which):
        sender = Sender(send)
        columns = (pl.ds(0, FIRST), pl.ds(FIRST, 3 * width - FIRST))
        ga = Gather(wqkv, all_rows, columns[which], sender, recv_a, pair.at[0])
        go = Gather(wo, own_half, slab, sender, recv_o, pair.at[1])
        gh = Gather(wh, own_half, every_h, sender, recv_h, pair.at[2])
        for load in own_a(which):
            load.wait()
        if which:
            ga.across()
        else:
            ga.column_begin()
        own_o.wait()
        go.across()
        own_h.wait()
        gh.across()
        ga.share(ga.block(0, 0))
        normalise()
        if which:
            chunk = (3 * width - FIRST) // 2
            chunks = [(pl.ds(FIRST + k * chunk, chunk), 3 + 7 * k) for k in range(2)]
            ga.crossed()
            for part in chunks:
                ga.ring_begin(*part)
            go.crossed()
            go.plane()
            for d in (1, 2, 3):
                ga.share(ga.block(0, -d))
            find_near()
            for s in (1, 2, 3, 4):
                for part in chunks:
                    ga.ring_step(*part, s)
                if s == 1:
                    go.planed()
                    go.y_begin()
                if s == 3:
                    go.y_step(1)
                    gh.crossed()
                    gh.plane()
        else:
            ga.column_step(1)
            go.crossed()
            go.plane()
            ga.column_pass(0)
            ga.column_step(2)
            find_near()
            ga.column_pass(1)
            go.planed()
            go.y_begin()
            ga.column_step(3)
            ga.column_pass(2)
            ga.column_step(4)
            ga.column_pass(3)
            gh.crossed()
            gh.plane()
            ga.column_pass(4)
            ga.column_end(0)
            go.y_step(1)
            ga.column_pass(5)
            ga.column_end(1)
            ga.column_pass(6)
            ga.column_end(2)
            ga.column_pass(7)
            for index in (3, 4, 5, 6, 7):
                ga.column_end(index)
        landed(wqkv.at[:, :, :, columns[1 - which]], pair.at[0])
        sender.finish()

    for which in range(2):
        @pl.when(core == which)
        def _():
            for load in own_a(which):
                load.start()

    own_o.start()
    own_h.start()
    for load in small:
        load.start()
    greet(all_peers())
    for which in range(2):
        @pl.when(core == which)
        def _():
            gather(which)

    sender = Sender(send, SENDS)
    go = Gather(wo, own_half, slab, sender, recv_o, pair.at[1])
    gh = Gather(wh, own_half, every_h, sender, recv_h, pair.at[2])

    before, after = (
        {"node": (node + NZ * NX - 1) % (NZ * NX)},
        {"node": (node + 1) % (NZ * NX)},
    )

    def halo(t, way):
        columns = lane(t * TILE, TILE)
        source, target_rows, peer = (
            (HALO, rows + HALO, before),
            (rows, 0, after),
        )[way]
        return pltpu.make_async_remote_copy(
            src_ref=kv.at[:, pl.ds(source, HALO), columns],
            dst_ref=kv.at[:, pl.ds(target_rows, HALO), columns],
            send_sem=halo_send.at[way, t],
            recv_sem=halo_recv.at[way, t],
            device_id=peer,
            device_id_type=MESH,
        )

    @pl.loop(0, width // TILE)
    def _(t):
        def product(base):
            columns = lane(base + t * TILE, TILE)
            return mat(normed[...], wqkv[:, :, :, columns].reshape(width, TILE))

        inner = pl.ds(HALO, rows)
        for base, unit, kept in ((0, q_unit, q_factor), (width, k_unit, k_factor)):
            full = product(base)
            for side in range(TILE // 128):
                part = full[:, side * 128 : side * 128 + 128]
                columns = lane(t * TILE + side * 128, 128)
                scale = lax.rsqrt(head_mean(part * part) + 1e-06)
                unit[:, columns] = part * scale
                kept[:, columns] = scale
                if base:
                    kv[0, inner, columns] = (part * scale).astype(half)
                else:
                    q_half[:, columns] = (part * scale).astype(half)
        kv[1, inner, lane(t * TILE, TILE)] = product(2 * width).astype(half)
        halo(t, 0).start()
        halo(t, 1).start()

    go.y_step(2)
    gh.planed()
    gh.share(wh.at[:, :, own_half])

    @pl.loop(0, width // TILE)
    def _(t):
        halo(t, 0).wait()
        halo(t, 1).wait()

    def attend(p):
        columns = lane(p * 128, 128)
        keys, held = kv[0, :, columns], kv[1, :, columns]
        mixed = []
        for side, query in enumerate(two_heads(q_half[:, columns])):
            raised = jnp.exp(mat_back(query, keys) * 0.125) * near[...]
            weight = raised / jnp.sum(raised, axis=1, keepdims=True)
            attention[2 * p + side] = weight
            mixed.append(mat(weight.astype(half), held))
        left[0, :, columns] = jnp.where(head_side(), mixed[0], mixed[1]).astype(half)

    pairs = width // 128
    pl.loop(0, pairs // 2, unroll=2)(attend)
    go.y_step(3)
    pl.loop(pairs // 2, pairs, unroll=2)(attend)

    twin = at(z, x, y, 1 - core)
    sender.start(left.at[0], left.at[1], recv_core.at[0], twin)
    go.y_step(4)
    landed(wo.at[:, :, pl.ds(0, 16)], pair.at[1])
    landed(wh.at[:, :, pl.ds(0, 16)], pair.at[2])
    small[3].wait()
    small[4].wait()

    @pl.loop(0, width // TILE)
    def _(t):
        columns = lane(t * TILE, TILE)
        product = mat(left[0], wo[:, :, :, columns].reshape(width, TILE))
        settled[:, columns] = (nodes[:, columns].astype(f32) + product).astype(half)

    error = mat(settled[...], wh[...].reshape(width, wh.shape[3])) - target[...]
    differ[...] = error
    differs[0] = error.astype(half)
    ens = y % 4
    for d in (1, 2, 3):
        peer = {"ens": (ens + d) % 4}
        sender.start(differs.at[0], differs.at[d], ens_recv.at[d - 1], peer)
    own_sign = soft_sign(error)
    paired = jnp.zeros_like(error)
    for d in (1, 2, 3):
        landed(differs.at[d], ens_recv.at[d - 1])
        paired = paired + soft_sign(error - differs[d].astype(f32))
    members = 4
    coefficient = fair_weight / (2 * members * (members - 1)) + (1 - fair_weight) / (
        2 * members * members
    )
    core_grad = own_sign / members - 2 * coefficient * paired
    weight = jnp.broadcast_to(area[...], (rows, rows)).T
    grad_pred = (weight * core_grad).astype(half)

    @pl.loop(0, width // TILE)
    def _(t):
        block = wh[pl.ds(2 * t, 2)].reshape(TILE, wh.shape[3])
        gs[:, lane(t * TILE, TILE)] = mat_back(grad_pred, block).astype(half)

    wide = width // 2
    mine, other = lane(core * wide, wide), lane((1 - core) * wide, wide)
    sender.start(gs.at[:, other], right.at[1], recv_core.at[1], twin)
    right[0] = gs[:, mine]

    @pl.loop(0, width // TILE)
    def _(t):
        block = wo[pl.ds(2 * t, 2)].reshape(TILE, width)
        gm[:, lane(t * TILE, TILE)] = mat_back(gs[...], block).astype(half)

    landed(left.at[1], recv_core.at[0])
    landed(right.at[1], recv_core.at[1])
    tall = width // NZ

    def by_x(block, d):
        return pltpu.make_async_remote_copy(
            src_ref=parts.at[block, (x + d) % NX],
            dst_ref=from_x.at[d - 1, block],
            send_sem=send_x.at[d - 1, block],
            recv_sem=recv_x.at[d - 1, block],
            device_id=at(z, (x + d) % NX, y, core),
            device_id_type=MESH,
        )

    @pl.loop(0, NZ)
    def _(block):
        columns = lane(block * tall, tall)
        total = mat_across(left[0, :, columns], right[0])
        total = total + mat_across(left[1, :, columns], right[1])
        parts[block] = total[:, :BY_X].astype(half).reshape(parts.shape[1:])
        parts_b[block] = total[:, BY_X:].astype(half).reshape(parts_b.shape[1:])
        for d in range(1, NX):
            by_x(block, d).start()

    for d in range(1, NZ):
        sender.start(
            parts_b.at[(z + d) % NZ],
            from_z_b.at[d - 1],
            recv_z_b.at[d - 1],
            at((z + d) % NZ, x, y, core),
        )

    for group in range(2):
        @pl.loop(group * 4, group * 4 + 4)
        def _(p):
            columns = lane(p * 128, 128)
            keys, held = kv[0, :, columns], kv[1, :, columns]
            grads = two_heads(gm[:, columns])
            queries = two_heads(q_half[:, columns])
            logits, halves_of, query_grad = [], [], []
            for side in range(2):
                weight = attention[2 * p + side]
                scores = mat_back(grads[side], held)
                mean = jnp.sum(weight * scores, axis=1, keepdims=True)
                logit = (weight * (scores - mean)).astype(half)
                logits.append(logit)
                halves_of.append(weight.astype(half))
                query_grad.append(mat(logit, keys))
            grad = jnp.where(head_side(), query_grad[0], query_grad[1]) * 0.125
            unit = q_unit[:, columns]
            gq[:, columns] = (
                q_factor[:, columns] * (grad - unit * head_mean(grad * unit))
            ).astype(half)
            key_grad = (
                mat_across(logits[0], queries[0]) + mat_across(logits[1], queries[1])
            ) * 0.125
            value_grad = mat_across(halves_of[0], grads[0]) + mat_across(
                halves_of[1], grads[1]
            )
            for k, (grad, kept) in enumerate(((key_grad, dk), (value_grad, dv))):
                kept[:, columns] = grad[HALO : HALO + rows]
                halo_out[0, k, :, columns] = grad[:HALO].astype(half)
                halo_out[1, k, :, columns] = grad[
                    HALO + rows : 2 * HALO + rows
                ].astype(half)

        columns = pl.ds(group * wide, wide)
        for way, peer in enumerate((before, after)):
            sender.start(
                halo_out.at[way, :, :, columns],
                halo_in.at[way, :, :, columns],
                back_recv.at[way, group],
                peer,
            )

    @pl.loop(0, width // TILE)
    def _(t):
        block = wqkv[pl.ds(2 * t, 2), :, :, pl.ds(0, width)].reshape(TILE, width)
        gn[:, lane(t * TILE, TILE)] = mat_back(gq[...], block)

    @pl.loop(0, NZ)
    def _(block):
        for d in range(1, NX):
            by_x(block, d).wait()

    total = parts[:, x].astype(f32)
    for d in range(1, NX):
        total = total + from_x[d - 1].astype(f32)
    halves[...] = total.astype(half)
    for d in range(1, NZ):
        sender.start(
            halves.at[(z + d) % NZ],
            from_z.at[d - 1],
            recv_z.at[d - 1],
            at((z + d) % NZ, x, y, core),
        )
    for d in range(1, NZ):
        landed(from_z_b.at[d - 1], recv_z_b.at[d - 1])
    total = parts_b[z].astype(f32)
    for d in range(1, NZ):
        total = total + from_z_b[d - 1].astype(f32)
    halves_b[...] = total.astype(half)
    for d in range(1, NX):
        sender.start(
            halves_b.at[(x + d) % NX],
            from_x_b.at[d - 1],
            recv_x_b.at[d - 1],
            at(z, (x + d) % NX, y, core),
        )

    for way in range(2):
        for group in range(2):
            region = halo_in.at[way, :, :, pl.ds(group * wide, wide)]
            landed(region, back_recv.at[way, group])
    for k, kept in enumerate((dk, dv)):
        low, high = pl.ds(0, HALO), pl.ds(rows - HALO, HALO)
        kept[low, :] = kept[low, :] + halo_in[1, k].astype(f32)
        kept[high, :] = kept[high, :] + halo_in[0, k].astype(f32)

    @pl.loop(0, width // 128)
    def _(p):
        columns = lane(p * 128, 128)
        grad, unit = dk[:, columns], k_unit[:, columns]
        gk[:, columns] = (
            k_factor[:, columns] * (grad - unit * head_mean(grad * unit))
        ).astype(half)
        gv[:, columns] = dv[:, columns].astype(half)

    @pl.loop(0, width // TILE)
    def _(t):
        columns = lane(t * TILE, TILE)
        blocks = wqkv.at[pl.ds(2 * t, 2)]
        keys = blocks[:, :, :, pl.ds(width, width)].reshape(TILE, width)
        held = blocks[:, :, :, pl.ds(2 * width, width)].reshape(TILE, width)
        gn[:, columns] = (
            gn[:, columns] + mat_back(gk[...], keys) + mat_back(gv[...], held)
        )

    @pl.loop(0, rows // 32)
    def _(t):
        block = pl.ds(pl.multiple_of(t * 32, 32), 32)
        grad, unit = gn[block, :], normal[block, :]
        centre = jnp.mean(grad, axis=1, keepdims=True)
        along = jnp.mean(grad * unit, axis=1, keepdims=True)
        change = factor[block, pl.ds(0, 1)] * (grad - centre - unit * along)
        out[block, :] = (gs[block, :].astype(f32) + change).astype(half)

    for d in range(1, NZ):
        landed(from_z.at[d - 1], recv_z.at[d - 1])
    total = halves[z].astype(f32)
    for d in range(1, NZ):
        total = total + from_z[d - 1].astype(f32)
    for d in range(1, NX):
        landed(from_x_b.at[d - 1], recv_x_b.at[d - 1])
    total_b = halves_b[x].astype(f32)
    for d in range(1, NX):
        total_b = total_b + from_x_b[d - 1].astype(f32)
    for k in range(pieces.shape[0]):
        pieces[k, :, :BY_X] = total[2 * k : 2 * k + 2, :]
        pieces[k, :, BY_X:] = total_b[2 * k : 2 * k + 2, :]
    for dc in range(2):
        for dy in range(NY):
            if dy or dc:
                to_y, to_core = (y + dy) % NY, (core + dc) % 2
                index = (to_y % 4) * 4 + (to_y // 4) * 2 + to_core
                slot = dc * NY + dy
                sender.start(
                    pieces.at[index],
                    from_y.at[slot],
                    recv_y.at[slot],
                    at(z, x, to_y, to_core),
                )
    for dc in range(2):
        total = jnp.zeros(pieces.shape[1:], f32)
        for dy in range(NY):
            slot = dc * NY + dy
            if slot:
                landed(from_y.at[slot], recv_y.at[slot])
                total = total + from_y[slot]
            else:
                total = total + pieces[(y % 4) * 4 + (y // 4) * 2 + core]
        per = wide // 128
        for i in range(total.shape[0]):
            for j in range(per):
                first = i * NY + (core + dc) % 2 * per + j
                out_sum[pl.ds(first, 1), :] = total[i : i + 1, j * 128 : j * 128 + 128]
    sender.finish()


def shards(
    nodes, w_query, w_key, w_value, w_output, w_head, neighbours, edge_counts, target, node_area
):
    rows, width = nodes.shape[2:]
    variables = w_head.shape[1]
    wide, block = width // 2, width // NZ // NX
    own = width // (NZ * NX * 2 * NY)
    f32, half = jnp.float32, jnp.bfloat16

    def vmem(shape, kind=half):
        return pltpu.VMEM(shape, kind)

    full = (rows, width)
    dma = pltpu.SemaphoreType.DMA
    scratch = [
        vmem(full),
        vmem((neighbours.shape[1], rows), jnp.int32),
        vmem((1, rows), jnp.int32),
        vmem((rows, variables), f32),
        vmem((1, rows), f32),
        vmem((NZ, NX, block, 3 * width)),
        vmem((NZ, NX, block, width)),
        vmem((NZ, NX, block, variables)),
        vmem(full, f32),
        vmem(full),
        vmem((rows, 128), f32),
        vmem(full, f32),
        vmem(full, f32),
        vmem(full, f32),
        vmem(full, f32),
        vmem(full),
        vmem((2, EXT, width)),
        vmem((rows, EXT), f32),
        vmem((HEADS, rows, EXT), f32),
        vmem((2, rows, width)),
        vmem((2, rows, wide)),
        vmem(full),
        vmem((rows, variables), f32),
        vmem((4, rows, variables)),
        vmem(full),
        vmem(full),
        vmem(full),
        vmem(full, f32),
        vmem(full, f32),
        vmem(full),
        vmem(full),
        vmem(full, f32),
        vmem((2, 2, HALO, width)),
        vmem((2, 2, HALO, width)),
        vmem((NZ, NX, block, BY_X)),
        vmem((NX - 1, NZ, block, BY_X)),
        vmem((NZ, block, BY_X)),
        vmem((NZ - 1, block, BY_X)),
        vmem((NZ, NX, block, wide - BY_X)),
        vmem((NZ - 1, NX, block, wide - BY_X)),
        vmem((NX, block, wide - BY_X)),
        vmem((NX - 1, block, wide - BY_X)),
        vmem((2 * NY, own, wide), f32),
        vmem((2 * NY, own, wide), f32),
        dma((9,)),
        dma((SENDS + 64,)),
        dma((31,)),
        dma((17,)),
        dma((10,)),
        dma((3,)),
        dma((2, width // TILE)),
        dma((2, width // TILE)),
        dma((2, 2)),
        dma((3,)),
        dma((2,)),
        dma((NX - 1, NZ)),
        dma((NX - 1, NZ)),
        dma((NZ - 1,)),
        dma((NX - 1,)),
        dma((NZ - 1,)),
        dma((2 * NY,)),
    ]
    inside = pl.BlockSpec(memory_space=pltpu.VMEM)
    outside = pl.BlockSpec(memory_space=pltpu.HBM)
    grad_nodes, grad_out_proj = pl.pallas_call(
        layer_kernel,
        out_shape=[
            jax.ShapeDtypeStruct(full, half),
            jax.ShapeDtypeStruct((own * NY, width // NY), f32),
        ],
        in_specs=[outside] * 10,
        out_specs=[inside, inside],
        scratch_shapes=scratch,
        compiler_params=pltpu.CompilerParams(
            collective_id=0, has_side_effects=True, vmem_limit_bytes=62 * 2**20
        ),
        name="layer",
    )(
        nodes.reshape(full),
        w_query,
        w_key,
        w_value,
        w_output,
        w_head,
        neighbours.T,
        edge_counts.reshape(1, rows),
        target.reshape(rows, variables),
        node_area.reshape(1, rows),
    )
    return grad_nodes.reshape(nodes.shape), grad_out_proj.reshape(-1)


def solution(mesh):
    placed = (
        P("dp", "ens", "node", None),
        P("node", None),
        P("node", None),
        P("node", None),
        P("node", None),
        P("node", None),
        P("node", None),
        P("node"),
        P("dp", "node", None),
        P("node"),
    )
    return jax.shard_map(
        shards,
        mesh=mesh,
        in_specs=placed,
        out_specs=(P("dp", "ens", "node", None), P(("node", "ens", "dp"))),
        check_vma=False,
    )
```

```python
import jax
import jax.numpy as jnp
from jax import lax
from jax.experimental import pallas as pl
from jax.experimental.pallas import tpu as pltpu
from jax.sharding import PartitionSpec as P

HEADS = 16


fair_weight = 0.95
soft_square = 0.25

NZ, NX, NY = 8, 4, 8
MESH = pl.DeviceIdType.MESH


def place():
    node = lax.axis_index("node")
    ens = lax.axis_index("ens")
    dp = lax.axis_index("dp")
    return node // NX, node % NX, (dp // 2) * 4 + ens, dp % 2


def at(z, x, y, core):
    return {"node": z * NX + x, "ens": y % 4, "dp": (y // 4) * 2 + core}


class Sender:
    def __init__(self, sems, first=0):
        self.sems, self.count, self.sent = sems, first, []

    def start(self, src, dst, recv_sem, device):
        copy = pltpu.make_async_remote_copy(
            src_ref=src,
            dst_ref=dst,
            send_sem=self.sems.at[self.count],
            recv_sem=recv_sem,
            device_id=device,
            device_id_type=MESH,
        )
        self.count += 1
        copy.start()
        self.sent.append(copy)

    def finish(self):
        for copy in self.sent:
            copy.wait_send()
        self.sent = []


def landed(region, sem):
    pltpu.make_async_copy(region, region, sem).wait()


def greet(peers):
    barrier = pltpu.get_barrier_semaphore()
    for peer in peers:
        pl.semaphore_signal(barrier, inc=1, device_id=peer, device_id_type=MESH)
    pl.semaphore_wait(barrier, len(peers))


TILE = 256
HALO = 32
EXT = 256
FIRST = 1792
BY_X = 384
STRAIGHT = (6, 7)
SENDS = 130
ORDER = (0, -1, 1, -2, 2, -3, 3, 4)


def spread(z):
    return (z + 2 * NZ) % NZ


class Gather:
    def __init__(self, whole, rows, columns, sender, recv, pair):
        self.whole, self.rows, self.columns = whole, rows, columns
        self.sender, self.recv, self.pair = sender, recv, pair
        z, x, y, core = place()
        self.z, self.x, self.y, self.core = z, x, y, core
        self.near = [at(z, (x + d) % NX, y, core) for d in (1, 2, 3)]
        self.up = at((z + 1) % NZ, x, y, core)
        self.down = at((z + NZ - 1) % NZ, x, y, core)
        self.twin = at(z, x, y, 1 - core)

    def send(self, region, sem, peer):
        self.sender.start(region, region, self.recv.at[sem], peer)

    def landed(self, region, sem):
        landed(region, self.recv.at[sem])

    def share(self, region):
        self.sender.start(region, region, self.pair, self.twin)

    def block(self, dz, dx, columns=None):
        z, x = spread(self.z + dz), (self.x + dx + NX) % NX
        return self.whole.at[z, x, self.rows, columns or self.columns]

    def line(self, dz, columns=None):
        return self.whole.at[
            spread(self.z + dz), :, self.rows, columns or self.columns
        ]


    def across(self, base=0):
        for d in range(3):
            self.send(self.block(0, 0), base + d, self.near[d])

    def crossed(self, base=0):
        for d in (1, 2, 3):
            self.landed(self.block(0, -d), base + d - 1)

    def ring_begin(self, columns, base):
        self.send(self.line(0, columns), base, self.up)
        self.send(self.line(0, columns), base + 4, self.down)

    def ring_step(self, columns, base, s):
        low, high = self.line(-s, columns), self.line(s, columns)
        self.landed(low, base + s - 1)
        if s < 4:
            self.send(low, base + s, self.up)
            self.landed(high, base + s + 3)
            if s < 3:
                self.send(high, base + s + 4, self.down)
        self.share(low)
        if s < 4:
            self.share(high)


    def fan(self, index):
        region = self.block(ORDER[index], 0)
        self.send(region, 7 + index, self.near[0])
        self.send(region, 15 + index, self.near[2])
        if index in STRAIGHT:
            self.send(region, 23 + index, self.near[1])

    def column_begin(self):
        self.send(self.block(0, 0), 0, self.up)
        self.send(self.block(0, 0), 4, self.down)
        self.fan(0)

    def column_step(self, s):
        low, high = self.block(-s, 0), self.block(s, 0)
        self.landed(low, s - 1)
        if s < 4:
            self.send(low, s, self.up)
        self.fan(ORDER.index(-s if s < 4 else 4))
        if s < 4:
            self.landed(high, s + 3)
            if s < 3:
                self.send(high, s + 4, self.down)
            self.fan(ORDER.index(s))
        self.share(low)
        if s < 4:
            self.share(high)

    def column_pass(self, index):
        for dx, base, onward in ((-1, 7, self.near[0]), (1, 15, self.near[2])):
            region = self.block(ORDER[index], dx)
            self.landed(region, base + index)
            if index not in STRAIGHT and (index % 2 == 0) == (dx < 0):
                self.send(region, 23 + index, onward)
            self.share(region)

    def column_end(self, index):
        region = self.block(ORDER[index], 2)
        self.landed(region, 23 + index)
        self.share(region)


    def plane(self):
        z, x, y, core = self.z, self.x, self.y, self.core
        for d in range(1, NZ):
            self.send(self.line(0), 2 + d, at((z + d) % NZ, x, y, core))

    def planed(self):
        for d in range(1, NZ):
            self.landed(self.line(-d), 2 + d)


    def slab(self, dy):
        width = self.whole.shape[3] // NY
        first = pl.multiple_of(((self.y + dy + NY) % NY) * width, width)
        return self.whole.at[:, :, self.rows, pl.ds(first, width)]

    def y_begin(self, base=10):
        z, x, y, core = self.z, self.x, self.y, self.core
        self.send(self.slab(0), base, at(z, x, (y + 1) % NY, core))
        self.send(self.slab(0), base + 4, at(z, x, (y + NY - 1) % NY, core))
        self.share(self.slab(0))

    def y_step(self, s, base=10):
        z, x, y, core = self.z, self.x, self.y, self.core
        low, high = self.slab(-s), self.slab(s)
        self.landed(low, base + s - 1)
        if s < 4:
            self.send(low, base + s, at(z, x, (y + 1) % NY, core))
            self.landed(high, base + s + 3)
            if s < 3:
                self.send(high, base + s + 4, at(z, x, (y + NY - 1) % NY, core))
        self.share(low)
        if s < 4:
            self.share(high)


def all_peers():
    z, x, y, core = place()
    node = z * NX + x
    peers = [at(z, (x + d) % NX, y, core) for d in range(1, NX)]
    peers += [at((z + d) % NZ, x, y, core) for d in range(1, NZ)]
    for dy in range(NY):
        for dc in range(2):
            if dy or dc:
                peers.append(at(z, x, (y + dy) % NY, (core + dc) % 2))
    peers.append({"node": (node + 1) % (NZ * NX)})
    peers.append({"node": (node + NZ * NX - 1) % (NZ * NX)})
    return peers


def mat(left, right):
    return jnp.dot(left, right, preferred_element_type=jnp.float32)


def mat_back(left, right):
    return lax.dot_general(
        left, right, (((1,), (1,)), ((), ())), preferred_element_type=jnp.float32
    )


def mat_across(left, right):
    return lax.dot_general(
        left, right, (((0,), (0,)), ((), ())), preferred_element_type=jnp.float32
    )


def soft_sign(values):
    return values * lax.rsqrt(values * values + soft_square)


def lane(start, size):
    return pl.ds(pl.multiple_of(start, size), size)


def head_side():
    return lax.broadcasted_iota(jnp.int32, (1, 128), 1) < 64


def head_mean(values):
    side = head_side()
    low = jnp.sum(jnp.where(side, values, 0.0), axis=1, keepdims=True)
    high = jnp.sum(jnp.where(side, 0.0, values), axis=1, keepdims=True)
    return jnp.where(side, low, high) * (1.0 / 64)


def two_heads(values):
    side = head_side()
    empty = jnp.zeros_like(values)
    return jnp.where(side, values, empty), jnp.where(side, empty, values)


def layer_kernel(
    nodes_in, wq_shard, wk_shard, wv_shard, wo_shard, wh_shard, neighbours_in,
    counts_in, target_in, area_in, out, out_sum,
    nodes, neighbours, counts, target, area,
    wqkv, wo, wh, normal, normed, factor, q_unit, k_unit, q_factor, k_factor, q_half,
    kv, near, attention, left, right, settled, differ, differs, gs, gm, gq, dk, dv,
    gk, gv, gn, halo_out, halo_in, parts, from_x, halves, from_z, parts_b, from_z_b,
    halves_b, from_x_b, pieces, from_y,
    local, send, recv_a, recv_o, recv_h, pair, halo_send, halo_recv, back_recv,
    ens_recv, recv_core, send_x, recv_x, recv_z, recv_x_b, recv_z_b, recv_y,
):
    f32, half = jnp.float32, jnp.bfloat16
    z, x, y, core = place()
    node = z * NX + x
    rows, width = nodes.shape
    small = [
        pltpu.make_async_copy(source, kept, local.at[k])
        for k, (source, kept) in enumerate(
            (
                (nodes_in, nodes),
                (neighbours_in, neighbours),
                (counts_in, counts),
                (target_in, target),
                (area_in, area),
            )
        )
    ]
    own_half = pl.ds(pl.multiple_of(core * 16, 16), 16)
    slab = pl.ds(pl.multiple_of(y * 128, 128), 128)
    every = pl.ds(0, width)
    every_h = pl.ds(0, wh_shard.shape[1])

    def own(k, shard, whole, taken_rows, taken, kept):
        return pltpu.make_async_copy(
            shard.at[taken_rows, taken],
            whole.at[z, x, taken_rows, kept],
            local.at[5 + k],
        )

    all_rows = pl.ds(0, wq_shard.shape[0])
    own_o = own(0, wo_shard, wo, own_half, slab, slab)
    own_h = own(1, wh_shard, wh, own_half, every_h, every_h)

    def own_a(which):
        rest = FIRST - width
        if which:
            end, kept = pl.ds(rest, width - rest), pl.ds(FIRST, width - rest)
            loads = [own(2, wv_shard, wqkv, all_rows, every, pl.ds(2 * width, width))]
            if rest < width:
                loads.append(own(3, wk_shard, wqkv, all_rows, end, kept))
            return loads
        start = pl.ds(0, rest)
        return [
            own(2, wq_shard, wqkv, all_rows, every, pl.ds(0, width)),
            own(3, wk_shard, wqkv, all_rows, start, pl.ds(width, rest)),
        ]

    def normalise():
        small[0].wait()
        values = nodes[...].astype(f32)
        shifted = values - jnp.mean(values, axis=1, keepdims=True)
        scale = lax.rsqrt(jnp.mean(shifted * shifted, axis=1, keepdims=True) + 1e-05)
        factor[...] = jnp.broadcast_to(scale, factor.shape)
        normal[...] = shifted * scale
        normed[...] = normal[...].astype(half)

    def find_near():
        small[1].wait()
        small[2].wait()
        total = NZ * NX * rows
        column = (neighbours[...] - node * rows + HALO + total) & (total - 1)
        at_column = lax.broadcasted_iota(jnp.int32, (EXT, rows), 0)
        hits = jnp.zeros((EXT, rows), f32)
        for s in range(neighbours.shape[0]):
            hit = (column[s : s + 1, :] == at_column) & (counts[...] > s)
            hits = hits + jnp.where(hit, 1.0, 0.0)
        near[...] = hits.T
        kv[:, pl.ds(rows + 2 * HALO, EXT - rows - 2 * HALO)] = jnp.zeros(
            (2, EXT - rows - 2 * HALO, width), half
        )

    def gather(which):
        sender = Sender(send)
        columns = (pl.ds(0, FIRST), pl.ds(FIRST, 3 * width - FIRST))
        ga = Gather(wqkv, all_rows, columns[which], sender, recv_a, pair.at[0])
        go = Gather(wo, own_half, slab, sender, recv_o, pair.at[1])
        gh = Gather(wh, own_half, every_h, sender, recv_h, pair.at[2])
        for load in own_a(which):
            load.wait()
        if which:
            ga.across()
        else:
            ga.column_begin()
        own_o.wait()
        go.across()
        own_h.wait()
        gh.across()
        ga.share(ga.block(0, 0))
        normalise()
        if which:
            chunk = (3 * width - FIRST) // 2
            chunks = [(pl.ds(FIRST + k * chunk, chunk), 3 + 7 * k) for k in range(2)]
            ga.crossed()
            for part in chunks:
                ga.ring_begin(*part)
            go.crossed()
            go.plane()
            for d in (1, 2, 3):
                ga.share(ga.block(0, -d))
            find_near()
            for s in (1, 2, 3, 4):
                for part in chunks:
                    ga.ring_step(*part, s)
                if s == 1:
                    go.planed()
                    go.y_begin()
                if s == 3:
                    go.y_step(1)
                    gh.crossed()
                    gh.plane()
        else:
            ga.column_step(1)
            go.crossed()
            go.plane()
            ga.column_pass(0)
            ga.column_step(2)
            find_near()
            ga.column_pass(1)
            go.planed()
            go.y_begin()
            ga.column_step(3)
            ga.column_pass(2)
            ga.column_step(4)
            ga.column_pass(3)
            gh.crossed()
            gh.plane()
            ga.column_pass(4)
            ga.column_end(0)
            go.y_step(1)
            ga.column_pass(5)
            ga.column_end(1)
            ga.column_pass(6)
            ga.column_end(2)
            ga.column_pass(7)
            for index in (3, 4, 5, 6, 7):
                ga.column_end(index)
        landed(wqkv.at[:, :, :, columns[1 - which]], pair.at[0])
        sender.finish()

    for which in range(2):
        @pl.when(core == which)
        def _():
            for load in own_a(which):
                load.start()

    own_o.start()
    own_h.start()
    for load in small:
        load.start()
    greet(all_peers())
    for which in range(2):
        @pl.when(core == which)
        def _():
            gather(which)

    sender = Sender(send, SENDS)
    go = Gather(wo, own_half, slab, sender, recv_o, pair.at[1])
    gh = Gather(wh, own_half, every_h, sender, recv_h, pair.at[2])

    before, after = (
        {"node": (node + NZ * NX - 1) % (NZ * NX)},
        {"node": (node + 1) % (NZ * NX)},
    )

    def halo(t, way):
        columns = lane(t * TILE, TILE)
        source, target_rows, peer = (
            (HALO, rows + HALO, before),
            (rows, 0, after),
        )[way]
        return pltpu.make_async_remote_copy(
            src_ref=kv.at[:, pl.ds(source, HALO), columns],
            dst_ref=kv.at[:, pl.ds(target_rows, HALO), columns],
            send_sem=halo_send.at[way, t],
            recv_sem=halo_recv.at[way, t],
            device_id=peer,
            device_id_type=MESH,
        )

    @pl.loop(0, width // TILE)
    def _(t):
        def product(base):
            columns = lane(base + t * TILE, TILE)
            return mat(normed[...], wqkv[:, :, :, columns].reshape(width, TILE))

        inner = pl.ds(HALO, rows)
        for base, unit, kept in ((0, q_unit, q_factor), (width, k_unit, k_factor)):
            full = product(base)
            for side in range(TILE // 128):
                part = full[:, side * 128 : side * 128 + 128]
                columns = lane(t * TILE + side * 128, 128)
                scale = lax.rsqrt(head_mean(part * part) + 1e-06)
                unit[:, columns] = part * scale
                kept[:, columns] = scale
                if base:
                    kv[0, inner, columns] = (part * scale).astype(half)
                else:
                    q_half[:, columns] = (part * scale).astype(half)
        kv[1, inner, lane(t * TILE, TILE)] = product(2 * width).astype(half)
        halo(t, 0).start()
        halo(t, 1).start()

    go.y_step(2)
    gh.planed()
    gh.share(wh.at[:, :, own_half])

    @pl.loop(0, width // TILE)
    def _(t):
        halo(t, 0).wait()
        halo(t, 1).wait()

    def attend(p):
        columns = lane(p * 128, 128)
        keys, held = kv[0, :, columns], kv[1, :, columns]
        mixed = []
        for side, query in enumerate(two_heads(q_half[:, columns])):
            raised = jnp.exp(mat_back(query, keys) * 0.125) * near[...]
            weight = raised / jnp.sum(raised, axis=1, keepdims=True)
            attention[2 * p + side] = weight
            mixed.append(mat(weight.astype(half), held))
        left[0, :, columns] = jnp.where(head_side(), mixed[0], mixed[1]).astype(half)

    pairs = width // 128
    pl.loop(0, pairs // 2, unroll=2)(attend)
    go.y_step(3)
    pl.loop(pairs // 2, pairs, unroll=2)(attend)

    twin = at(z, x, y, 1 - core)
    sender.start(left.at[0], left.at[1], recv_core.at[0], twin)
    go.y_step(4)
    landed(wo.at[:, :, pl.ds(0, 16)], pair.at[1])
    landed(wh.at[:, :, pl.ds(0, 16)], pair.at[2])
    small[3].wait()
    small[4].wait()

    @pl.loop(0, width // TILE)
    def _(t):
        columns = lane(t * TILE, TILE)
        product = mat(left[0], wo[:, :, :, columns].reshape(width, TILE))
        settled[:, columns] = (nodes[:, columns].astype(f32) + product).astype(half)

    error = mat(settled[...], wh[...].reshape(width, wh.shape[3])) - target[...]
    differ[...] = error
    differs[0] = error.astype(half)
    ens = y % 4
    for d in (1, 2, 3):
        peer = {"ens": (ens + d) % 4}
        sender.start(differs.at[0], differs.at[d], ens_recv.at[d - 1], peer)
    own_sign = soft_sign(error)
    paired = jnp.zeros_like(error)
    for d in (1, 2, 3):
        landed(differs.at[d], ens_recv.at[d - 1])
        paired = paired + soft_sign(error - differs[d].astype(f32))
    members = 4
    coefficient = fair_weight / (2 * members * (members - 1)) + (1 - fair_weight) / (
        2 * members * members
    )
    core_grad = own_sign / members - 2 * coefficient * paired
    weight = jnp.broadcast_to(area[...], (rows, rows)).T
    grad_pred = (weight * core_grad).astype(half)

    @pl.loop(0, width // TILE)
    def _(t):
        block = wh[pl.ds(2 * t, 2)].reshape(TILE, wh.shape[3])
        gs[:, lane(t * TILE, TILE)] = mat_back(grad_pred, block).astype(half)

    wide = width // 2
    mine, other = lane(core * wide, wide), lane((1 - core) * wide, wide)
    sender.start(gs.at[:, other], right.at[1], recv_core.at[1], twin)
    right[0] = gs[:, mine]

    @pl.loop(0, width // TILE)
    def _(t):
        block = wo[pl.ds(2 * t, 2)].reshape(TILE, width)
        gm[:, lane(t * TILE, TILE)] = mat_back(gs[...], block).astype(half)

    landed(left.at[1], recv_core.at[0])
    landed(right.at[1], recv_core.at[1])
    tall = width // NZ

    def by_x(block, d):
        return pltpu.make_async_remote_copy(
            src_ref=parts.at[block, (x + d) % NX],
            dst_ref=from_x.at[d - 1, block],
            send_sem=send_x.at[d - 1, block],
            recv_sem=recv_x.at[d - 1, block],
            device_id=at(z, (x + d) % NX, y, core),
            device_id_type=MESH,
        )

    @pl.loop(0, NZ)
    def _(block):
        columns = lane(block * tall, tall)
        total = mat_across(left[0, :, columns], right[0])
        total = total + mat_across(left[1, :, columns], right[1])
        parts[block] = total[:, :BY_X].astype(half).reshape(parts.shape[1:])
        parts_b[block] = total[:, BY_X:].astype(half).reshape(parts_b.shape[1:])
        for d in range(1, NX):
            by_x(block, d).start()

    for d in range(1, NZ):
        sender.start(
            parts_b.at[(z + d) % NZ],
            from_z_b.at[d - 1],
            recv_z_b.at[d - 1],
            at((z + d) % NZ, x, y, core),
        )

    for group in range(2):
        @pl.loop(group * 4, group * 4 + 4, unroll=2)
        def _(p):
            columns = lane(p * 128, 128)
            keys, held = kv[0, :, columns], kv[1, :, columns]
            grads = two_heads(gm[:, columns])
            queries = two_heads(q_half[:, columns])
            logits, halves_of, query_grad = [], [], []
            for side in range(2):
                weight = attention[2 * p + side]
                scores = mat_back(grads[side], held)
                mean = jnp.sum(weight * scores, axis=1, keepdims=True)
                logit = (weight * (scores - mean)).astype(half)
                logits.append(logit)
                halves_of.append(weight.astype(half))
                query_grad.append(mat(logit, keys))
            grad = jnp.where(head_side(), query_grad[0], query_grad[1]) * 0.125
            unit = q_unit[:, columns]
            gq[:, columns] = (
                q_factor[:, columns] * (grad - unit * head_mean(grad * unit))
            ).astype(half)
            key_grad = (
                mat_across(logits[0], queries[0]) + mat_across(logits[1], queries[1])
            ) * 0.125
            value_grad = mat_across(halves_of[0], grads[0]) + mat_across(
                halves_of[1], grads[1]
            )
            for k, (grad, kept) in enumerate(((key_grad, dk), (value_grad, dv))):
                kept[:, columns] = grad[HALO : HALO + rows]
                halo_out[0, k, :, columns] = grad[:HALO].astype(half)
                halo_out[1, k, :, columns] = grad[
                    HALO + rows : 2 * HALO + rows
                ].astype(half)

        columns = pl.ds(group * wide, wide)
        for way, peer in enumerate((before, after)):
            sender.start(
                halo_out.at[way, :, :, columns],
                halo_in.at[way, :, :, columns],
                back_recv.at[way, group],
                peer,
            )

    @pl.loop(0, NZ)
    def _(block):
        for d in range(1, NX):
            by_x(block, d).wait()

    total = parts[:, x].astype(f32)
    for d in range(1, NX):
        total = total + from_x[d - 1].astype(f32)
    halves[...] = total.astype(half)
    for d in range(1, NZ):
        sender.start(
            halves.at[(z + d) % NZ],
            from_z.at[d - 1],
            recv_z.at[d - 1],
            at((z + d) % NZ, x, y, core),
        )
    @pl.loop(0, width // TILE)
    def _(t):
        block = wqkv[pl.ds(2 * t, 2), :, :, pl.ds(0, width)].reshape(TILE, width)
        gn[:, lane(t * TILE, TILE)] = mat_back(gq[...], block)

    for d in range(1, NZ):
        landed(from_z_b.at[d - 1], recv_z_b.at[d - 1])
    total = parts_b[z].astype(f32)
    for d in range(1, NZ):
        total = total + from_z_b[d - 1].astype(f32)
    halves_b[...] = total.astype(half)
    for d in range(1, NX):
        sender.start(
            halves_b.at[(x + d) % NX],
            from_x_b.at[d - 1],
            recv_x_b.at[d - 1],
            at(z, (x + d) % NX, y, core),
        )

    for way in range(2):
        for group in range(2):
            region = halo_in.at[way, :, :, pl.ds(group * wide, wide)]
            landed(region, back_recv.at[way, group])
    for k, kept in enumerate((dk, dv)):
        low, high = pl.ds(0, HALO), pl.ds(rows - HALO, HALO)
        kept[low, :] = kept[low, :] + halo_in[1, k].astype(f32)
        kept[high, :] = kept[high, :] + halo_in[0, k].astype(f32)

    @pl.loop(0, width // 128)
    def _(p):
        columns = lane(p * 128, 128)
        grad, unit = dk[:, columns], k_unit[:, columns]
        gk[:, columns] = (
            k_factor[:, columns] * (grad - unit * head_mean(grad * unit))
        ).astype(half)
        gv[:, columns] = dv[:, columns].astype(half)

    @pl.loop(0, width // TILE)
    def _(t):
        columns = lane(t * TILE, TILE)
        blocks = wqkv.at[pl.ds(2 * t, 2)]
        keys = blocks[:, :, :, pl.ds(width, width)].reshape(TILE, width)
        held = blocks[:, :, :, pl.ds(2 * width, width)].reshape(TILE, width)
        gn[:, columns] = (
            gn[:, columns] + mat_back(gk[...], keys) + mat_back(gv[...], held)
        )

    @pl.loop(0, rows // 32)
    def _(t):
        block = pl.ds(pl.multiple_of(t * 32, 32), 32)
        grad, unit = gn[block, :], normal[block, :]
        centre = jnp.mean(grad, axis=1, keepdims=True)
        along = jnp.mean(grad * unit, axis=1, keepdims=True)
        change = factor[block, pl.ds(0, 1)] * (grad - centre - unit * along)
        out[block, :] = (gs[block, :].astype(f32) + change).astype(half)

    for d in range(1, NZ):
        landed(from_z.at[d - 1], recv_z.at[d - 1])
    total = halves[z].astype(f32)
    for d in range(1, NZ):
        total = total + from_z[d - 1].astype(f32)
    for d in range(1, NX):
        landed(from_x_b.at[d - 1], recv_x_b.at[d - 1])
    total_b = halves_b[x].astype(f32)
    for d in range(1, NX):
        total_b = total_b + from_x_b[d - 1].astype(f32)
    for k in range(pieces.shape[0]):
        pieces[k, :, :BY_X] = total[2 * k : 2 * k + 2, :]
        pieces[k, :, BY_X:] = total_b[2 * k : 2 * k + 2, :]
    for dc in range(2):
        for dy in range(NY):
            if dy or dc:
                to_y, to_core = (y + dy) % NY, (core + dc) % 2
                index = (to_y % 4) * 4 + (to_y // 4) * 2 + to_core
                slot = dc * NY + dy
                sender.start(
                    pieces.at[index],
                    from_y.at[slot],
                    recv_y.at[slot],
                    at(z, x, to_y, to_core),
                )
    for dc in range(2):
        total = jnp.zeros(pieces.shape[1:], f32)
        for dy in range(NY):
            slot = dc * NY + dy
            if slot:
                landed(from_y.at[slot], recv_y.at[slot])
                total = total + from_y[slot]
            else:
                total = total + pieces[(y % 4) * 4 + (y // 4) * 2 + core]
        per = wide // 128
        for i in range(total.shape[0]):
            for j in range(per):
                first = i * NY + (core + dc) % 2 * per + j
                out_sum[pl.ds(first, 1), :] = total[i : i + 1, j * 128 : j * 128 + 128]
    sender.finish()


def shards(
    nodes, w_query, w_key, w_value, w_output, w_head, neighbours, edge_counts, target, node_area
):
    rows, width = nodes.shape[2:]
    variables = w_head.shape[1]
    wide, block = width // 2, width // NZ // NX
    own = width // (NZ * NX * 2 * NY)
    f32, half = jnp.float32, jnp.bfloat16

    def vmem(shape, kind=half):
        return pltpu.VMEM(shape, kind)

    full = (rows, width)
    dma = pltpu.SemaphoreType.DMA
    scratch = [
        vmem(full),
        vmem((neighbours.shape[1], rows), jnp.int32),
        vmem((1, rows), jnp.int32),
        vmem((rows, variables), f32),
        vmem((1, rows), f32),
        vmem((NZ, NX, block, 3 * width)),
        vmem((NZ, NX, block, width)),
        vmem((NZ, NX, block, variables)),
        vmem(full, f32),
        vmem(full),
        vmem((rows, 128), f32),
        vmem(full, f32),
        vmem(full, f32),
        vmem(full, f32),
        vmem(full, f32),
        vmem(full),
        vmem((2, EXT, width)),
        vmem((rows, EXT), f32),
        vmem((HEADS, rows, EXT), f32),
        vmem((2, rows, width)),
        vmem((2, rows, wide)),
        vmem(full),
        vmem((rows, variables), f32),
        vmem((4, rows, variables)),
        vmem(full),
        vmem(full),
        vmem(full),
        vmem(full, f32),
        vmem(full, f32),
        vmem(full),
        vmem(full),
        vmem(full, f32),
        vmem((2, 2, HALO, width)),
        vmem((2, 2, HALO, width)),
        vmem((NZ, NX, block, BY_X)),
        vmem((NX - 1, NZ, block, BY_X)),
        vmem((NZ, block, BY_X)),
        vmem((NZ - 1, block, BY_X)),
        vmem((NZ, NX, block, wide - BY_X)),
        vmem((NZ - 1, NX, block, wide - BY_X)),
        vmem((NX, block, wide - BY_X)),
        vmem((NX - 1, block, wide - BY_X)),
        vmem((2 * NY, own, wide), f32),
        vmem((2 * NY, own, wide), f32),
        dma((9,)),
        dma((SENDS + 64,)),
        dma((31,)),
        dma((17,)),
        dma((10,)),
        dma((3,)),
        dma((2, width // TILE)),
        dma((2, width // TILE)),
        dma((2, 2)),
        dma((3,)),
        dma((2,)),
        dma((NX - 1, NZ)),
        dma((NX - 1, NZ)),
        dma((NZ - 1,)),
        dma((NX - 1,)),
        dma((NZ - 1,)),
        dma((2 * NY,)),
    ]
    inside = pl.BlockSpec(memory_space=pltpu.VMEM)
    outside = pl.BlockSpec(memory_space=pltpu.HBM)
    grad_nodes, grad_out_proj = pl.pallas_call(
        layer_kernel,
        out_shape=[
            jax.ShapeDtypeStruct(full, half),
            jax.ShapeDtypeStruct((own * NY, width // NY), f32),
        ],
        in_specs=[outside] * 10,
        out_specs=[inside, inside],
        scratch_shapes=scratch,
        compiler_params=pltpu.CompilerParams(
            collective_id=0, has_side_effects=True, vmem_limit_bytes=62 * 2**20
        ),
        name="layer",
    )(
        nodes.reshape(full),
        w_query,
        w_key,
        w_value,
        w_output,
        w_head,
        neighbours.T,
        edge_counts.reshape(1, rows),
        target.reshape(rows, variables),
        node_area.reshape(1, rows),
    )
    return grad_nodes.reshape(nodes.shape), grad_out_proj.reshape(-1)


def solution(mesh):
    placed = (
        P("dp", "ens", "node", None),
        P("node", None),
        P("node", None),
        P("node", None),
        P("node", None),
        P("node", None),
        P("node", None),
        P("node"),
        P("dp", "node", None),
        P("node"),
    )
    return jax.shard_map(
        shards,
        mesh=mesh,
        in_specs=placed,
        out_specs=(P("dp", "ens", "node", None), P(("node", "ens", "dp"))),
        check_vma=False,
    )
```

```python
import jax
import jax.numpy as jnp
from jax import lax
from jax.experimental import pallas as pl
from jax.experimental.pallas import tpu as pltpu
from jax.sharding import PartitionSpec as P

HEADS = 16


fair_weight = 0.95
soft_square = 0.25

NZ, NX, NY = 8, 4, 8
MESH = pl.DeviceIdType.MESH


def place():
    node = lax.axis_index("node")
    ens = lax.axis_index("ens")
    dp = lax.axis_index("dp")
    return node // NX, node % NX, (dp // 2) * 4 + ens, dp % 2


def at(z, x, y, core):
    return {"node": z * NX + x, "ens": y % 4, "dp": (y // 4) * 2 + core}


class Sender:
    def __init__(self, sems, first=0):
        self.sems, self.count, self.sent = sems, first, []

    def start(self, src, dst, recv_sem, device):
        copy = pltpu.make_async_remote_copy(
            src_ref=src,
            dst_ref=dst,
            send_sem=self.sems.at[self.count],
            recv_sem=recv_sem,
            device_id=device,
            device_id_type=MESH,
        )
        self.count += 1
        copy.start()
        self.sent.append(copy)

    def finish(self):
        for copy in self.sent:
            copy.wait_send()
        self.sent = []


def landed(region, sem):
    pltpu.make_async_copy(region, region, sem).wait()


def greet(peers):
    barrier = pltpu.get_barrier_semaphore()
    for peer in peers:
        pl.semaphore_signal(barrier, inc=1, device_id=peer, device_id_type=MESH)
    pl.semaphore_wait(barrier, len(peers))


TILE = 256
HALO = 32
EXT = 256
FIRST = 1792
BY_X = 384
STRAIGHT = (6, 7)
SENDS = 130
ORDER = (0, -1, 1, -2, 2, -3, 3, 4)


def spread(z):
    return (z + 2 * NZ) % NZ


class Gather:
    def __init__(self, whole, rows, columns, sender, recv, pair):
        self.whole, self.rows, self.columns = whole, rows, columns
        self.sender, self.recv, self.pair = sender, recv, pair
        z, x, y, core = place()
        self.z, self.x, self.y, self.core = z, x, y, core
        self.near = [at(z, (x + d) % NX, y, core) for d in (1, 2, 3)]
        self.up = at((z + 1) % NZ, x, y, core)
        self.down = at((z + NZ - 1) % NZ, x, y, core)
        self.twin = at(z, x, y, 1 - core)

    def send(self, region, sem, peer):
        self.sender.start(region, region, self.recv.at[sem], peer)

    def landed(self, region, sem):
        landed(region, self.recv.at[sem])

    def share(self, region):
        self.sender.start(region, region, self.pair, self.twin)

    def block(self, dz, dx, columns=None):
        z, x = spread(self.z + dz), (self.x + dx + NX) % NX
        return self.whole.at[z, x, self.rows, columns or self.columns]

    def line(self, dz, columns=None):
        return self.whole.at[
            spread(self.z + dz), :, self.rows, columns or self.columns
        ]


    def across(self, base=0):
        for d in range(3):
            self.send(self.block(0, 0), base + d, self.near[d])

    def crossed(self, base=0):
        for d in (1, 2, 3):
            self.landed(self.block(0, -d), base + d - 1)

    def ring_begin(self, columns, base):
        self.send(self.line(0, columns), base, self.up)
        self.send(self.line(0, columns), base + 4, self.down)

    def ring_step(self, columns, base, s):
        low, high = self.line(-s, columns), self.line(s, columns)
        self.landed(low, base + s - 1)
        if s < 4:
            self.send(low, base + s, self.up)
            self.landed(high, base + s + 3)
            if s < 3:
                self.send(high, base + s + 4, self.down)
        self.share(low)
        if s < 4:
            self.share(high)


    def fan(self, index):
        region = self.block(ORDER[index], 0)
        self.send(region, 7 + index, self.near[0])
        self.send(region, 15 + index, self.near[2])
        if index in STRAIGHT:
            self.send(region, 23 + index, self.near[1])

    def column_begin(self):
        self.send(self.block(0, 0), 0, self.up)
        self.send(self.block(0, 0), 4, self.down)
        self.fan(0)

    def column_step(self, s):
        low, high = self.block(-s, 0), self.block(s, 0)
        self.landed(low, s - 1)
        if s < 4:
            self.send(low, s, self.up)
        self.fan(ORDER.index(-s if s < 4 else 4))
        if s < 4:
            self.landed(high, s + 3)
            if s < 3:
                self.send(high, s + 4, self.down)
            self.fan(ORDER.index(s))
        self.share(low)
        if s < 4:
            self.share(high)

    def column_pass(self, index):
        for dx, base, onward in ((-1, 7, self.near[0]), (1, 15, self.near[2])):
            region = self.block(ORDER[index], dx)
            self.landed(region, base + index)
            if index not in STRAIGHT and (index % 2 == 0) == (dx < 0):
                self.send(region, 23 + index, onward)
            self.share(region)

    def column_end(self, index):
        region = self.block(ORDER[index], 2)
        self.landed(region, 23 + index)
        self.share(region)


    def plane(self):
        z, x, y, core = self.z, self.x, self.y, self.core
        for d in range(1, NZ):
            self.send(self.line(0), 2 + d, at((z + d) % NZ, x, y, core))

    def planed(self):
        for d in range(1, NZ):
            self.landed(self.line(-d), 2 + d)


    def slab(self, dy):
        width = self.whole.shape[3] // NY
        first = pl.multiple_of(((self.y + dy + NY) % NY) * width, width)
        return self.whole.at[:, :, self.rows, pl.ds(first, width)]

    def y_begin(self, base=10):
        z, x, y, core = self.z, self.x, self.y, self.core
        self.send(self.slab(0), base, at(z, x, (y + 1) % NY, core))
        self.send(self.slab(0), base + 4, at(z, x, (y + NY - 1) % NY, core))
        self.share(self.slab(0))

    def y_step(self, s, base=10):
        z, x, y, core = self.z, self.x, self.y, self.core
        low, high = self.slab(-s), self.slab(s)
        self.landed(low, base + s - 1)
        if s < 4:
            self.send(low, base + s, at(z, x, (y + 1) % NY, core))
            self.landed(high, base + s + 3)
            if s < 3:
                self.send(high, base + s + 4, at(z, x, (y + NY - 1) % NY, core))
        self.share(low)
        if s < 4:
            self.share(high)


def all_peers():
    z, x, y, core = place()
    node = z * NX + x
    peers = [at(z, (x + d) % NX, y, core) for d in range(1, NX)]
    peers += [at((z + d) % NZ, x, y, core) for d in range(1, NZ)]
    for dy in range(NY):
        for dc in range(2):
            if dy or dc:
                peers.append(at(z, x, (y + dy) % NY, (core + dc) % 2))
    peers.append({"node": (node + 1) % (NZ * NX)})
    peers.append({"node": (node + NZ * NX - 1) % (NZ * NX)})
    return peers


def mat(left, right):
    return jnp.dot(left, right, preferred_element_type=jnp.float32)


def mat_back(left, right):
    return lax.dot_general(
        left, right, (((1,), (1,)), ((), ())), preferred_element_type=jnp.float32
    )


def mat_across(left, right):
    return lax.dot_general(
        left, right, (((0,), (0,)), ((), ())), preferred_element_type=jnp.float32
    )


def soft_sign(values):
    return values * lax.rsqrt(values * values + soft_square)


def lane(start, size):
    return pl.ds(pl.multiple_of(start, size), size)


def head_side():
    return lax.broadcasted_iota(jnp.int32, (1, 128), 1) < 64


def head_mean(values):
    side = head_side()
    low = jnp.sum(jnp.where(side, values, 0.0), axis=1, keepdims=True)
    high = jnp.sum(jnp.where(side, 0.0, values), axis=1, keepdims=True)
    return jnp.where(side, low, high) * (1.0 / 64)


def two_heads(values):
    side = head_side()
    empty = jnp.zeros_like(values)
    return jnp.where(side, values, empty), jnp.where(side, empty, values)


def layer_kernel(
    nodes_in, wq_shard, wk_shard, wv_shard, wo_shard, wh_shard, neighbours_in,
    counts_in, target_in, area_in, out, out_sum,
    nodes, neighbours, counts, target, area,
    wqkv, wo, wh, normal, normed, factor, q_unit, k_unit, q_factor, k_factor, q_half,
    kv, near, attention, left, right, settled, differ, differs, gs, gm, gq, dk, dv,
    gk, gv, gn, halo_out, halo_in, parts, from_x, halves, from_z, parts_b, from_z_b,
    halves_b, from_x_b, pieces, from_y,
    local, send, recv_a, recv_o, recv_h, pair, halo_send, halo_recv, back_recv,
    ens_recv, recv_core, send_x, recv_x, recv_z, recv_x_b, recv_z_b, recv_y,
):
    f32, half = jnp.float32, jnp.bfloat16
    z, x, y, core = place()
    node = z * NX + x
    rows, width = nodes.shape
    small = [
        pltpu.make_async_copy(source, kept, local.at[k])
        for k, (source, kept) in enumerate(
            (
                (nodes_in, nodes),
                (neighbours_in, neighbours),
                (counts_in, counts),
                (target_in, target),
                (area_in, area),
            )
        )
    ]
    own_half = pl.ds(pl.multiple_of(core * 16, 16), 16)
    slab = pl.ds(pl.multiple_of(y * 128, 128), 128)
    every = pl.ds(0, width)
    every_h = pl.ds(0, wh_shard.shape[1])

    def own(k, shard, whole, taken_rows, taken, kept):
        return pltpu.make_async_copy(
            shard.at[taken_rows, taken],
            whole.at[z, x, taken_rows, kept],
            local.at[5 + k],
        )

    all_rows = pl.ds(0, wq_shard.shape[0])
    own_o = own(0, wo_shard, wo, own_half, slab, slab)
    own_h = own(1, wh_shard, wh, own_half, every_h, every_h)

    def own_a(which):
        rest = FIRST - width
        if which:
            end, kept = pl.ds(rest, width - rest), pl.ds(FIRST, width - rest)
            loads = [own(2, wv_shard, wqkv, all_rows, every, pl.ds(2 * width, width))]
            if rest < width:
                loads.append(own(3, wk_shard, wqkv, all_rows, end, kept))
            return loads
        start = pl.ds(0, rest)
        return [
            own(2, wq_shard, wqkv, all_rows, every, pl.ds(0, width)),
            own(3, wk_shard, wqkv, all_rows, start, pl.ds(width, rest)),
        ]

    def normalise():
        small[0].wait()
        values = nodes[...].astype(f32)
        shifted = values - jnp.mean(values, axis=1, keepdims=True)
        scale = lax.rsqrt(jnp.mean(shifted * shifted, axis=1, keepdims=True) + 1e-05)
        factor[...] = jnp.broadcast_to(scale, factor.shape)
        normal[...] = shifted * scale
        normed[...] = normal[...].astype(half)

    def find_near():
        small[1].wait()
        small[2].wait()
        total = NZ * NX * rows
        column = (neighbours[...] - node * rows + HALO + total) & (total - 1)
        at_column = lax.broadcasted_iota(jnp.int32, (EXT, rows), 0)
        hits = jnp.zeros((EXT, rows), f32)
        for s in range(neighbours.shape[0]):
            hit = (column[s : s + 1, :] == at_column) & (counts[...] > s)
            hits = hits + jnp.where(hit, 1.0, 0.0)
        near[...] = hits.T
        kv[:, pl.ds(rows + 2 * HALO, EXT - rows - 2 * HALO)] = jnp.zeros(
            (2, EXT - rows - 2 * HALO, width), half
        )

    def gather(which):
        sender = Sender(send)
        columns = (pl.ds(0, FIRST), pl.ds(FIRST, 3 * width - FIRST))
        ga = Gather(wqkv, all_rows, columns[which], sender, recv_a, pair.at[0])
        go = Gather(wo, own_half, slab, sender, recv_o, pair.at[1])
        gh = Gather(wh, own_half, every_h, sender, recv_h, pair.at[2])
        for load in own_a(which):
            load.wait()
        if which:
            ga.across()
        else:
            ga.column_begin()
        own_o.wait()
        go.across()
        own_h.wait()
        gh.across()
        ga.share(ga.block(0, 0))
        normalise()
        if which:
            chunk = (3 * width - FIRST) // 2
            chunks = [(pl.ds(FIRST + k * chunk, chunk), 3 + 7 * k) for k in range(2)]
            ga.crossed()
            for part in chunks:
                ga.ring_begin(*part)
            go.crossed()
            go.plane()
            for d in (1, 2, 3):
                ga.share(ga.block(0, -d))
            find_near()
            for s in (1, 2, 3, 4):
                for part in chunks:
                    ga.ring_step(*part, s)
                if s == 1:
                    go.planed()
                    go.y_begin()
                if s == 3:
                    go.y_step(1)
                    gh.crossed()
                    gh.plane()
        else:
            ga.column_step(1)
            go.crossed()
            go.plane()
            ga.column_pass(0)
            ga.column_step(2)
            find_near()
            ga.column_pass(1)
            go.planed()
            go.y_begin()
            ga.column_step(3)
            ga.column_pass(2)
            ga.column_step(4)
            ga.column_pass(3)
            gh.crossed()
            gh.plane()
            ga.column_pass(4)
            ga.column_end(0)
            go.y_step(1)
            ga.column_pass(5)
            ga.column_end(1)
            ga.column_pass(6)
            ga.column_end(2)
            ga.column_pass(7)
            for index in (3, 4, 5, 6, 7):
                ga.column_end(index)
        landed(wqkv.at[:, :, :, columns[1 - which]], pair.at[0])
        sender.finish()

    for which in range(2):
        @pl.when(core == which)
        def _():
            for load in own_a(which):
                load.start()

    own_o.start()
    own_h.start()
    for load in small:
        load.start()
    greet(all_peers())
    for which in range(2):
        @pl.when(core == which)
        def _():
            gather(which)

    sender = Sender(send, SENDS)
    go = Gather(wo, own_half, slab, sender, recv_o, pair.at[1])
    gh = Gather(wh, own_half, every_h, sender, recv_h, pair.at[2])

    before, after = (
        {"node": (node + NZ * NX - 1) % (NZ * NX)},
        {"node": (node + 1) % (NZ * NX)},
    )

    def halo(t, way):
        columns = lane(t * TILE, TILE)
        source, target_rows, peer = (
            (HALO, rows + HALO, before),
            (rows, 0, after),
        )[way]
        return pltpu.make_async_remote_copy(
            src_ref=kv.at[:, pl.ds(source, HALO), columns],
            dst_ref=kv.at[:, pl.ds(target_rows, HALO), columns],
            send_sem=halo_send.at[way, t],
            recv_sem=halo_recv.at[way, t],
            device_id=peer,
            device_id_type=MESH,
        )

    @pl.loop(0, width // TILE)
    def _(t):
        def product(base):
            columns = lane(base + t * TILE, TILE)
            return mat(normed[...], wqkv[:, :, :, columns].reshape(width, TILE))

        inner = pl.ds(HALO, rows)
        for base, unit, kept in ((0, q_unit, q_factor), (width, k_unit, k_factor)):
            full = product(base)
            for side in range(TILE // 128):
                part = full[:, side * 128 : side * 128 + 128]
                columns = lane(t * TILE + side * 128, 128)
                scale = lax.rsqrt(head_mean(part * part) + 1e-06)
                unit[:, columns] = part * scale
                kept[:, columns] = scale
                if base:
                    kv[0, inner, columns] = (part * scale).astype(half)
                else:
                    q_half[:, columns] = (part * scale).astype(half)
        kv[1, inner, lane(t * TILE, TILE)] = product(2 * width).astype(half)
        halo(t, 0).start()
        halo(t, 1).start()

    go.y_step(2)
    gh.planed()
    gh.share(wh.at[:, :, own_half])

    @pl.loop(0, width // TILE)
    def _(t):
        halo(t, 0).wait()
        halo(t, 1).wait()

    def attend(p):
        columns = lane(p * 128, 128)
        keys, held = kv[0, :, columns], kv[1, :, columns]
        mixed = []
        for side, query in enumerate(two_heads(q_half[:, columns])):
            raised = jnp.exp(mat_back(query, keys) * 0.125) * near[...]
            weight = raised / jnp.sum(raised, axis=1, keepdims=True)
            attention[2 * p + side] = weight
            mixed.append(mat(weight.astype(half), held))
        left[0, :, columns] = jnp.where(head_side(), mixed[0], mixed[1]).astype(half)

    pairs = width // 128
    pl.loop(0, pairs // 2, unroll=2)(attend)
    go.y_step(3)
    pl.loop(pairs // 2, pairs, unroll=2)(attend)

    twin = at(z, x, y, 1 - core)
    sender.start(left.at[0], left.at[1], recv_core.at[0], twin)
    go.y_step(4)
    landed(wo.at[:, :, pl.ds(0, 16)], pair.at[1])
    landed(wh.at[:, :, pl.ds(0, 16)], pair.at[2])
    small[3].wait()
    small[4].wait()

    @pl.loop(0, width // TILE)
    def _(t):
        columns = lane(t * TILE, TILE)
        product = mat(left[0], wo[:, :, :, columns].reshape(width, TILE))
        settled[:, columns] = (nodes[:, columns].astype(f32) + product).astype(half)

    error = mat(settled[...], wh[...].reshape(width, wh.shape[3])) - target[...]
    differ[...] = error
    differs[0] = error.astype(half)
    ens = y % 4
    for d in (1, 2, 3):
        peer = {"ens": (ens + d) % 4}
        sender.start(differs.at[0], differs.at[d], ens_recv.at[d - 1], peer)
    own_sign = soft_sign(error)
    paired = jnp.zeros_like(error)
    for d in (1, 2, 3):
        landed(differs.at[d], ens_recv.at[d - 1])
        paired = paired + soft_sign(error - differs[d].astype(f32))
    members = 4
    coefficient = fair_weight / (2 * members * (members - 1)) + (1 - fair_weight) / (
        2 * members * members
    )
    core_grad = own_sign / members - 2 * coefficient * paired
    weight = jnp.broadcast_to(area[...], (rows, rows)).T
    grad_pred = (weight * core_grad).astype(half)

    @pl.loop(0, width // TILE)
    def _(t):
        block = wh[pl.ds(2 * t, 2)].reshape(TILE, wh.shape[3])
        gs[:, lane(t * TILE, TILE)] = mat_back(grad_pred, block).astype(half)

    wide = width // 2
    mine, other = lane(core * wide, wide), lane((1 - core) * wide, wide)
    sender.start(gs.at[:, other], right.at[1], recv_core.at[1], twin)
    right[0] = gs[:, mine]

    @pl.loop(0, width // TILE)
    def _(t):
        block = wo[pl.ds(2 * t, 2)].reshape(TILE, width)
        gm[:, lane(t * TILE, TILE)] = mat_back(gs[...], block).astype(half)

    landed(left.at[1], recv_core.at[0])
    landed(right.at[1], recv_core.at[1])
    tall = width // NZ

    def by_x(block, d):
        return pltpu.make_async_remote_copy(
            src_ref=parts.at[block, (x + d) % NX],
            dst_ref=from_x.at[d - 1, block],
            send_sem=send_x.at[d - 1, block],
            recv_sem=recv_x.at[d - 1, block],
            device_id=at(z, (x + d) % NX, y, core),
            device_id_type=MESH,
        )

    @pl.loop(0, NZ)
    def _(block):
        columns = lane(block * tall, tall)
        total = mat_across(left[0, :, columns], right[0])
        total = total + mat_across(left[1, :, columns], right[1])
        parts[block] = total[:, :BY_X].astype(half).reshape(parts.shape[1:])
        parts_b[block] = total[:, BY_X:].astype(half).reshape(parts_b.shape[1:])
        for d in range(1, NX):
            by_x(block, d).start()

    for d in range(1, NZ):
        sender.start(
            parts_b.at[(z + d) % NZ],
            from_z_b.at[d - 1],
            recv_z_b.at[d - 1],
            at((z + d) % NZ, x, y, core),
        )

    for group in range(2):
        @pl.loop(group * 4, group * 4 + 4, unroll=2)
        def _(p):
            columns = lane(p * 128, 128)
            keys, held = kv[0, :, columns], kv[1, :, columns]
            grads = two_heads(gm[:, columns])
            queries = two_heads(q_half[:, columns])
            logits, halves_of, query_grad = [], [], []
            for side in range(2):
                weight = attention[2 * p + side]
                scores = mat_back(grads[side], held)
                mean = jnp.sum(weight * scores, axis=1, keepdims=True)
                logit = (weight * (scores - mean)).astype(half)
                logits.append(logit)
                halves_of.append(weight.astype(half))
                query_grad.append(mat(logit, keys))
            grad = jnp.where(head_side(), query_grad[0], query_grad[1]) * 0.125
            unit = q_unit[:, columns]
            gq[:, columns] = (
                q_factor[:, columns] * (grad - unit * head_mean(grad * unit))
            ).astype(half)
            key_grad = (
                mat_across(logits[0], queries[0]) + mat_across(logits[1], queries[1])
            ) * 0.125
            value_grad = mat_across(halves_of[0], grads[0]) + mat_across(
                halves_of[1], grads[1]
            )
            for k, (grad, kept) in enumerate(((key_grad, dk), (value_grad, dv))):
                kept[:, columns] = grad[HALO : HALO + rows]
                halo_out[0, k, :, columns] = grad[:HALO].astype(half)
                halo_out[1, k, :, columns] = grad[
                    HALO + rows : 2 * HALO + rows
                ].astype(half)

        columns = pl.ds(group * wide, wide)
        for way, peer in enumerate((before, after)):
            sender.start(
                halo_out.at[way, :, :, columns],
                halo_in.at[way, :, :, columns],
                back_recv.at[way, group],
                peer,
            )

    @pl.loop(0, NZ)
    def _(block):
        for d in range(1, NX):
            by_x(block, d).wait()

    total = parts[:, x].astype(f32)
    for d in range(1, NX):
        total = total + from_x[d - 1].astype(f32)
    halves[...] = total.astype(half)
    for d in range(1, NZ):
        sender.start(
            halves.at[(z + d) % NZ],
            from_z.at[d - 1],
            recv_z.at[d - 1],
            at((z + d) % NZ, x, y, core),
        )
    @pl.loop(0, width // TILE)
    def _(t):
        block = wqkv[pl.ds(2 * t, 2), :, :, pl.ds(0, width)].reshape(TILE, width)
        gn[:, lane(t * TILE, TILE)] = mat_back(gq[...], block)

    for d in range(1, NZ):
        landed(from_z_b.at[d - 1], recv_z_b.at[d - 1])
    total = parts_b[z].astype(f32)
    for d in range(1, NZ):
        total = total + from_z_b[d - 1].astype(f32)
    halves_b[...] = total.astype(half)
    for d in range(1, NX):
        sender.start(
            halves_b.at[(x + d) % NX],
            from_x_b.at[d - 1],
            recv_x_b.at[d - 1],
            at(z, (x + d) % NX, y, core),
        )

    for way in range(2):
        for group in range(2):
            region = halo_in.at[way, :, :, pl.ds(group * wide, wide)]
            landed(region, back_recv.at[way, group])
    for k, kept in enumerate((dk, dv)):
        low, high = pl.ds(0, HALO), pl.ds(rows - HALO, HALO)
        kept[low, :] = kept[low, :] + halo_in[1, k].astype(f32)
        kept[high, :] = kept[high, :] + halo_in[0, k].astype(f32)

    @pl.loop(0, width // 128)
    def _(p):
        columns = lane(p * 128, 128)
        grad, unit = dk[:, columns], k_unit[:, columns]
        gk[:, columns] = (
            k_factor[:, columns] * (grad - unit * head_mean(grad * unit))
        ).astype(half)
        gv[:, columns] = dv[:, columns].astype(half)

    @pl.loop(0, width // TILE)
    def _(t):
        columns = lane(t * TILE, TILE)
        blocks = wqkv.at[pl.ds(2 * t, 2)]
        keys = blocks[:, :, :, pl.ds(width, width)].reshape(TILE, width)
        held = blocks[:, :, :, pl.ds(2 * width, width)].reshape(TILE, width)
        gn[:, columns] = (
            gn[:, columns] + mat_back(gk[...], keys) + mat_back(gv[...], held)
        )

    @pl.loop(0, rows // 32)
    def _(t):
        block = pl.ds(pl.multiple_of(t * 32, 32), 32)
        grad, unit = gn[block, :], normal[block, :]
        centre = jnp.mean(grad, axis=1, keepdims=True)
        along = jnp.mean(grad * unit, axis=1, keepdims=True)
        change = factor[block, pl.ds(0, 1)] * (grad - centre - unit * along)
        out[block, :] = gs[block, :].astype(f32) + change

    for d in range(1, NZ):
        landed(from_z.at[d - 1], recv_z.at[d - 1])
    total = halves[z].astype(f32)
    for d in range(1, NZ):
        total = total + from_z[d - 1].astype(f32)
    for d in range(1, NX):
        landed(from_x_b.at[d - 1], recv_x_b.at[d - 1])
    total_b = halves_b[x].astype(f32)
    for d in range(1, NX):
        total_b = total_b + from_x_b[d - 1].astype(f32)
    for k in range(pieces.shape[0]):
        pieces[k, :, :BY_X] = total[2 * k : 2 * k + 2, :]
        pieces[k, :, BY_X:] = total_b[2 * k : 2 * k + 2, :]
    for dc in range(2):
        for dy in range(NY):
            if dy or dc:
                to_y, to_core = (y + dy) % NY, (core + dc) % 2
                index = (to_y % 4) * 4 + (to_y // 4) * 2 + to_core
                slot = dc * NY + dy
                sender.start(
                    pieces.at[index],
                    from_y.at[slot],
                    recv_y.at[slot],
                    at(z, x, to_y, to_core),
                )
    for dc in range(2):
        total = jnp.zeros(pieces.shape[1:], f32)
        for dy in range(NY):
            slot = dc * NY + dy
            if slot:
                landed(from_y.at[slot], recv_y.at[slot])
                total = total + from_y[slot]
            else:
                total = total + pieces[(y % 4) * 4 + (y // 4) * 2 + core]
        per = wide // 128
        for i in range(total.shape[0]):
            for j in range(per):
                first = i * NY + (core + dc) % 2 * per + j
                out_sum[pl.ds(first, 1), :] = total[i : i + 1, j * 128 : j * 128 + 128]
    sender.finish()


def shards(
    nodes, w_query, w_key, w_value, w_output, w_head, neighbours, edge_counts, target, node_area
):
    rows, width = nodes.shape[2:]
    variables = w_head.shape[1]
    wide, block = width // 2, width // NZ // NX
    own = width // (NZ * NX * 2 * NY)
    f32, half = jnp.float32, jnp.bfloat16

    def vmem(shape, kind=half):
        return pltpu.VMEM(shape, kind)

    full = (rows, width)
    dma = pltpu.SemaphoreType.DMA
    scratch = [
        vmem(full),
        vmem((neighbours.shape[1], rows), jnp.int32),
        vmem((1, rows), jnp.int32),
        vmem((rows, variables), f32),
        vmem((1, rows), f32),
        vmem((NZ, NX, block, 3 * width)),
        vmem((NZ, NX, block, width)),
        vmem((NZ, NX, block, variables)),
        vmem(full, f32),
        vmem(full),
        vmem((rows, 128), f32),
        vmem(full, f32),
        vmem(full, f32),
        vmem(full, f32),
        vmem(full, f32),
        vmem(full),
        vmem((2, EXT, width)),
        vmem((rows, EXT), f32),
        vmem((HEADS, rows, EXT), f32),
        vmem((2, rows, width)),
        vmem((2, rows, wide)),
        vmem(full),
        vmem((rows, variables), f32),
        vmem((4, rows, variables)),
        vmem(full),
        vmem(full),
        vmem(full),
        vmem(full, f32),
        vmem(full, f32),
        vmem(full),
        vmem(full),
        vmem(full, f32),
        vmem((2, 2, HALO, width)),
        vmem((2, 2, HALO, width)),
        vmem((NZ, NX, block, BY_X)),
        vmem((NX - 1, NZ, block, BY_X)),
        vmem((NZ, block, BY_X)),
        vmem((NZ - 1, block, BY_X)),
        vmem((NZ, NX, block, wide - BY_X)),
        vmem((NZ - 1, NX, block, wide - BY_X)),
        vmem((NX, block, wide - BY_X)),
        vmem((NX - 1, block, wide - BY_X)),
        vmem((2 * NY, own, wide), f32),
        vmem((2 * NY, own, wide), f32),
        dma((9,)),
        dma((SENDS + 64,)),
        dma((31,)),
        dma((17,)),
        dma((10,)),
        dma((3,)),
        dma((2, width // TILE)),
        dma((2, width // TILE)),
        dma((2, 2)),
        dma((3,)),
        dma((2,)),
        dma((NX - 1, NZ)),
        dma((NX - 1, NZ)),
        dma((NZ - 1,)),
        dma((NX - 1,)),
        dma((NZ - 1,)),
        dma((2 * NY,)),
    ]
    inside = pl.BlockSpec(memory_space=pltpu.VMEM)
    outside = pl.BlockSpec(memory_space=pltpu.HBM)
    grad_nodes, grad_out_proj = pl.pallas_call(
        layer_kernel,
        out_shape=[
            jax.ShapeDtypeStruct(full, f32),
            jax.ShapeDtypeStruct((own * NY, width // NY), f32),
        ],
        in_specs=[outside] * 10,
        out_specs=[inside, inside],
        scratch_shapes=scratch,
        compiler_params=pltpu.CompilerParams(
            collective_id=0, has_side_effects=True, vmem_limit_bytes=62 * 2**20
        ),
        name="layer",
    )(
        nodes.reshape(full),
        w_query,
        w_key,
        w_value,
        w_output,
        w_head,
        neighbours.T,
        edge_counts.reshape(1, rows),
        target.reshape(rows, variables),
        node_area.reshape(1, rows),
    )
    return grad_nodes.astype(half).reshape(nodes.shape), grad_out_proj.reshape(-1)


def solution(mesh):
    placed = (
        P("dp", "ens", "node", None),
        P("node", None),
        P("node", None),
        P("node", None),
        P("node", None),
        P("node", None),
        P("node", None),
        P("node"),
        P("dp", "node", None),
        P("node"),
    )
    return jax.shard_map(
        shards,
        mesh=mesh,
        in_specs=placed,
        out_specs=(P("dp", "ens", "node", None), P(("node", "ens", "dp"))),
        check_vma=False,
    )
```
